768 devices in a mesh: lon: 16 (over x, y_lo), lat: 48 (over z, y_hi, core).
Axes of the slice: x: 4, y: 8 (y_hi: 2, y_lo: 4; y = y_hi * 4 + y_lo), z: 12, core: 2. Of those that a mesh axis runs over, the one named last changes fastest.
Arguments:
- cotangent: float32 [2, 16, 1536, 4096], P(None, None, 'lat', 'lon'), may hold values from -6 to 6
- east_velocity: float32 [16, 1536, 4096], P(None, 'lat', 'lon'), may hold values from -1.8 to 1.8
- north_velocity: float32 [16, 1536, 4096], P(None, 'lat', 'lon'), may hold values from -1.8 to 1.8
- diffusivity: float32 [16, 1536, 4096], P(None, 'lat', 'lon'), may hold values from 0.02 to 0.12
- vertical_diffusivity: float32 [16, 1536, 4096], P(None, 'lat', 'lon'), may hold values from 0.02 to 0.2
- cell_mask: int32 [1536, 4096], P('lat', 'lon'), may hold values from 0 to 65535, as said below
- east_mask: int32 [1536, 4096], P('lat', 'lon'), may hold values from 0 to 65535, as said below
- north_mask: int32 [1536, 4096], P('lat', 'lon'), may hold values from 0 to 65535, as said below
- fold_partner: int32 [4096], P('lon'), may hold values from 0 to 4095, as said below
Outputs:
- initial_adjoint: float32 [2, 16, 1536, 4096], P(None, None, 'lat', 'lon')
The draws below stay inside these ranges and needn't reach their ends.
Inputs may be any that keep to these rules, and one draw needn't show every extreme that they name: `cell_mask`: bit k is set for the sea levels of a column, which run from level 0 down to a bottom level; land columns are 0. `east_mask`: equals cell_mask of the cell AND cell_mask of the next column, periodic in longitude. `north_mask`: equals cell_mask of the cell AND cell_mask of the next row; on the last row AND cell_mask of the last row at column fold_partner[i]. fold_partner[i] = (c - i) mod 4096 for one whole number c, so fold_partner[fold_partner[i]] = i.
All inputs are finite; a program needn't handle non-finite values.
Results may differ from the reference program's by a relative error of at most 0.0003.
Values sent between devices are 32-bit elements; how exact they have to be, the bound alone decides.
A program may use at most 64 MiB of HBM per device.

```python
import math
import jax
import jax.numpy as jnp
from jax import lax

LEV = 16
STEPS = 2
NLAT = 1536
NLON = 4096


def ocean_layout(key):
    depth_levels = jax.random.randint(jax.random.fold_in(key, 101), (NLAT, NLON), 1, LEV + 1)
    land_column = jax.random.randint(jax.random.fold_in(key, 102), (NLAT, NLON), 0, 5) == 0
    bottom = jnp.where(land_column, 0, depth_levels).astype(jnp.int32)
    cell_words = (jnp.left_shift(jnp.ones_like(bottom), bottom) - 1).astype(jnp.int32)
    offset = jax.random.randint(jax.random.fold_in(key, 103), (), 0, NLON)
    partner = jnp.mod(offset - jnp.arange(NLON, dtype=jnp.int32), NLON).astype(jnp.int32)
    east_words = jnp.bitwise_and(cell_words, jnp.roll(cell_words, -1, axis=1))
    above_words = jnp.concatenate([cell_words[1:], jnp.take(cell_words[-1:], partner, axis=1)], axis=0)
    north_words = jnp.bitwise_and(cell_words, above_words)
    return (cell_words, east_words.astype(jnp.int32), north_words.astype(jnp.int32), partner)


def draw_cell_mask(key, part):
    return ocean_layout(key)[0]


def draw_east_mask(key, part):
    return ocean_layout(key)[1]


def draw_north_mask(key, part):
    return ocean_layout(key)[2]


def draw_fold_partner(key, part):
    return ocean_layout(key)[3]


def block_levels(stream_key, shape, cuts, least, high):
    gain, own = 1.0, jax.random.fold_in(stream_key, 6)
    for axis_at, blocks in cuts:
        draws = jnp.exp(jax.random.uniform(jax.random.fold_in(own, axis_at), (blocks,), jnp.float32, least / len(cuts), high / len(cuts)))
        gain = gain * jnp.repeat(draws, shape[axis_at] // blocks).reshape([-1 if axis == axis_at else 1 for axis in range(len(shape))])
    return gain


def bell_draw(key, shape, width, limit, pieces=(), kind=jnp.bfloat16):
    drawn = width * jax.random.normal(key, shape, jnp.float32)
    if pieces:
        drawn = drawn * block_levels(key, shape, pieces, -0.22, 0.18)
    return jnp.clip(drawn, -limit, limit).astype(kind)


def setup_inputs(seed: int = 0) -> dict:
    arg_keys = jax.random.split(jax.random.key(seed), 10)
    cotangent = bell_draw(arg_keys[0], (2, LEV, NLAT, NLON), 1.0, 6.0, ((2, 48), (3, 16)), jnp.float32)
    east_velocity = bell_draw(arg_keys[1], (LEV, NLAT, NLON), 0.3, 1.8, ((1, 48), (2, 16)), jnp.float32)
    north_velocity = bell_draw(arg_keys[2], (LEV, NLAT, NLON), 0.3, 1.8, ((1, 48), (2, 16)), jnp.float32)
    diffusivity = jnp.clip(jnp.exp(math.log(0.12) - 1.7917595 * jax.random.uniform(arg_keys[3], (LEV, NLAT, NLON), jnp.float32) ** block_levels(arg_keys[3], (LEV, NLAT, NLON), ((1, 48), (2, 16)), -0.2, 0.2)), 0.02, 0.12)
    vertical_diffusivity = jnp.clip(jnp.exp(math.log(0.2) - 2.3025851 * jax.random.uniform(arg_keys[4], (LEV, NLAT, NLON), jnp.float32) ** block_levels(arg_keys[4], (LEV, NLAT, NLON), ((1, 48), (2, 16)), -0.2, 0.2)), 0.02, 0.2)
    cell_mask = draw_cell_mask(jax.random.fold_in(arg_keys[9], 71), 0)
    east_mask = draw_east_mask(jax.random.fold_in(arg_keys[9], 71), 0)
    north_mask = draw_north_mask(jax.random.fold_in(arg_keys[9], 71), 0)
    fold_partner = draw_fold_partner(jax.random.fold_in(arg_keys[9], 71), 0)
    return {"cotangent": cotangent, "east_velocity": east_velocity, "north_velocity": north_velocity, "diffusivity": diffusivity, "vertical_diffusivity": vertical_diffusivity, "cell_mask": cell_mask, "east_mask": east_mask, "north_mask": north_mask, "fold_partner": fold_partner}


def unpack_levels(packed_words, levels):
    level_bits = jnp.arange(levels, dtype=jnp.int32)[:, None, None]
    return jnp.bitwise_and(jnp.right_shift(packed_words[None], level_bits), 1).astype(jnp.float32)


def adjoint_step(incoming, operator_parts):
    cell_open, east_plus, east_minus, north_plus, north_minus, vertical, fold_partner = operator_parts
    masked = cell_open * incoming
    east_diff = jnp.roll(masked, -1, axis=2) - masked
    result = masked + east_plus * east_diff + jnp.roll(east_minus * east_diff, 1, axis=2)
    zero_row = jnp.zeros_like(masked[:, :1, :])
    north_diff = jnp.concatenate([masked[:, 1:, :], zero_row], axis=1) - masked
    north_push = north_minus * north_diff
    fold_back = jnp.take(north_push[:, -1:, :], fold_partner, axis=2)
    result = result + north_plus * north_diff + jnp.concatenate([zero_row, north_push[:, :-1, :]], axis=1)
    result = result + jnp.concatenate([jnp.zeros_like(masked[:, 1:, :]), fold_back], axis=1)
    level_flux = vertical * (masked[1:] - masked[:-1])
    zero_level = jnp.zeros_like(masked[:1])
    return result + jnp.concatenate([level_flux, zero_level], axis=0) - jnp.concatenate([zero_level, level_flux], axis=0)


def reference(cotangent, east_velocity, north_velocity, diffusivity, vertical_diffusivity, cell_mask, east_mask, north_mask, fold_partner):
    cell_open = unpack_levels(cell_mask, LEV)
    east_open = unpack_levels(east_mask, LEV)
    north_open = unpack_levels(north_mask, LEV)
    east_plus = east_open * (0.5 * east_velocity + diffusivity)
    east_minus = east_open * (0.5 * east_velocity - diffusivity)
    north_plus = north_open * (0.5 * north_velocity + diffusivity)
    north_minus = north_open * (0.5 * north_velocity - diffusivity)
    vertical = vertical_diffusivity[:-1] * cell_open[:-1] * cell_open[1:]
    operator_parts = (cell_open, east_plus, east_minus, north_plus, north_minus, vertical, fold_partner.astype(jnp.int32))

    def all_steps(tracer):
        for repeat in range(STEPS):
            tracer = adjoint_step(tracer, operator_parts)
        return tracer

    return lax.map(all_steps, cotangent)
```

```python
import functools

import jax
import jax.numpy as jnp
from jax import lax
from jax.experimental import pallas as pl
from jax.experimental.pallas import tpu as pltpu
from jax.sharding import PartitionSpec as P

LANES = 128
PAD = 8
UNROLL = 4


def loop_levels(levels, body):
    def trip(i, carry):
        for j in range(UNROLL):
            body(i * UNROLL + j)
        return carry

    lax.fori_loop(0, levels // UNROLL, trip, 0)


def kernel(
    n_lon, n_lat,
    ct, u_hbm, v_hbm, d_hbm, w_hbm, cm_hbm, em_hbm, nm_hbm, fp_hbm,
    out,
    a0, a1, nmb, ub, vb, db, wb, cmb, emb, nkb, fps,
    east_c, west_c, north_c, diag_c, down_c,
    send_e, send_w, recv_w, recv_e,
    fq, fg, fx, fy, fo, fb,
    load_sem, send_sem, recv_sem, fold_send, fold_recv,
):
    _, levels, rows, cols = ct.shape
    lon, lat = lax.axis_index("lon"), lax.axis_index("lat")
    east, west = lax.rem(lon + 1, n_lon), lax.rem(lon + n_lon - 1, n_lon)
    is_top, is_bottom = lat == n_lat - 1, lat == 0
    row_tiles = rows // 8
    first, last = PAD, PAD + rows - 1

    barrier = pltpu.get_barrier_semaphore()

    def greet(at):
        pl.semaphore_signal(barrier, inc=1, device_id=at, device_id_type=pl.DeviceIdType.MESH)

    @pl.when(is_top)
    def _():
        def one(p, carry):
            @pl.when(p != lon)
            def _():
                greet((p, lat))
            return carry
        lax.fori_loop(0, n_lon, one, 0)

    @pl.when(jnp.logical_not(is_top))
    def _():
        greet((east, lat))
        greet((west, lat))
        greet((lon, lat + 1))

    @pl.when(jnp.logical_not(is_bottom))
    def _():
        greet((lon, lat - 1))

    loads = []

    def load(src, dst):
        copy = pltpu.make_async_copy(src, dst, load_sem.at[len(loads)])
        copy.start()
        loads.append(copy)
        return copy

    ct_loads = [
        load(
            ct.at[:, :, :, pl.ds(LANES * l, LANES)],
            a0.at[:, pl.ds(1, levels), l, pl.ds(PAD, rows), :],
        )
        for l in range(2)
    ]
    coef_loads = [
        load(cm_hbm, cmb), load(nm_hbm, nkb), load(em_hbm, emb),
        load(d_hbm, db), load(v_hbm, vb), load(u_hbm, ub), load(w_hbm, wb), load(fp_hbm, fps),
    ]

    zeros = jnp.zeros((rows, LANES), jnp.float32)
    for buf in (a0, a1):
        for t in range(2):
            for k in (0, levels + 1):
                for l in range(2):
                    buf[t, k, l, pl.ds(PAD, rows), :] = zeros
    for l in range(2):
        down_c[0, :, LANES * l : LANES * (l + 1)] = zeros

    line = jnp.zeros((1, LANES), jnp.float32)

    @pl.when(is_bottom)
    def _():
        for k in range(levels):
            for l in range(2):
                nmb[k, l, pl.ds(first - 1, 1), :] = line
                for t in range(2):
                    a0[t, k + 1, l, pl.ds(first - 1, 1), :] = line
                    a1[t, k + 1, l, pl.ds(first - 1, 1), :] = line

    @pl.when(is_top)
    def _():
        for k in range(levels):
            for l in range(2):
                for t in range(2):
                    a0[t, k + 1, l, pl.ds(last + 1, 1), :] = line
                    a1[t, k + 1, l, pl.ds(last + 1, 1), :] = line

    lane = lax.broadcasted_iota(jnp.int32, (8, LANES), 1)
    at_first, at_last = lane == 0, lane == LANES - 1

    def moved(value, by):
        return pltpu.roll(value, by, 1)

    def pack_columns(src, dst, l, from_lane):
        def trip(i, acc):
            acc = list(acc)
            for j in range(UNROLL):
                k = i * UNROLL + j
                for t in range(2):
                    q = t * levels + k
                    for r in range(row_tiles):
                        value = src[t, k + 1, l, pl.ds(PAD + 8 * r, 8), :]
                        acc[r] = jnp.where(lane == q, moved(value, lax.rem(q + LANES - from_lane, LANES)), acc[r])
            return tuple(acc)

        acc = lax.fori_loop(
            0, levels // UNROLL, trip, tuple(jnp.zeros((8, LANES), jnp.float32) for _ in range(row_tiles))
        )
        for r in range(row_tiles):
            dst[pl.ds(8 * r, 8), :] = acc[r]

    for copy in ct_loads:
        copy.wait()
    pack_columns(a0, send_w.at[0], 0, 0)
    pack_columns(a0, send_e.at[0], 1, LANES - 1)
    for copy in coef_loads:
        copy.wait()

    zero = jnp.zeros((8, LANES), jnp.float32)

    def coefficients(k):
        bit = jnp.left_shift(jnp.int32(1), k)
        for r in range(row_tiles):
            rr = pl.ds(8 * r, 8)
            faces = []
            for l in range(2):
                cc = slice(LANES * l, LANES * (l + 1))
                half, diff = 0.5 * ub[k, rr, cc], db[k, rr, cc]
                open_e = jnp.bitwise_and(emb[rr, cc], bit) != 0
                plus = jnp.where(open_e, half + diff, 0.0)
                faces.append(jnp.where(open_e, half - diff, 0.0))
                east_c[k, rr, cc] = plus
                half = 0.5 * vb[k, rr, cc]
                open_n = jnp.bitwise_and(nkb[rr, cc], bit) != 0
                north = jnp.where(open_n, half + diff, 0.0)
                north_c[k, rr, cc] = north
                nmb[k, l, pl.ds(PAD + 8 * r, 8), :] = jnp.where(open_n, half - diff, 0.0)
                cells = cmb[rr, cc]
                both = jnp.left_shift(jnp.int32(3), k)
                down = jnp.where(jnp.bitwise_and(cells, both) == both, wb[k, rr, cc], 0.0)
                down_c[k + 1, rr, cc] = down
                here = jnp.where(jnp.bitwise_and(cells, bit) != 0, 1.0, 0.0)
                diag_c[k, rr, cc] = here - plus - north - down - down_c[k, rr, cc]
            turned = [moved(face, 1) for face in faces]
            west_c[k, rr, 0:LANES] = jnp.where(at_first, 0.0, turned[0])
            west_c[k, rr, LANES:cols] = jnp.where(at_first, turned[0], turned[1])
            to = 2 * levels + k
            send_e[0, rr, :] = jnp.where(
                lane == to, moved(faces[1], lax.rem(to + 1, LANES)), send_e[0, rr, :]
            )

    loop_levels(levels, coefficients)

    count = 2 + jnp.where(is_top, n_lon - 3, 1) + jnp.where(is_bottom, 0, 1)
    pl.semaphore_wait(barrier, count)

    def remote(src, dst, sem, at):
        return pltpu.make_async_remote_copy(
            src_ref=src, dst_ref=dst, send_sem=send_sem.at[sem], recv_sem=recv_sem.at[sem],
            device_id=at, device_id_type=pl.DeviceIdType.MESH,
        )

    def exchange(step, buf):
        base = 4 * step
        span = pl.ds(1, levels)
        to_east = remote(send_e.at[step], recv_w.at[step], base, (east, lat))
        to_west = remote(send_w.at[step], recv_e.at[step], base + 1, (west, lat))
        to_north = remote(
            buf.at[:, span, :, last, :], buf.at[:, span, :, first - 1, :], base + 2, (lon, lat + 1)
        )
        to_south = remote(
            buf.at[:, span, :, first, :], buf.at[:, span, :, last + 1, :], base + 3, (lon, lat - 1)
        )
        return to_east, to_west, to_north, to_south

    faces_north = remote(nmb.at[:, :, last, :], nmb.at[:, :, first - 1, :], 8, (lon, lat + 1))

    def start_exchange(copies):
        copies[0].start()
        copies[1].start()

        @pl.when(jnp.logical_not(is_top))
        def _():
            copies[2].start()

        @pl.when(jnp.logical_not(is_bottom))
        def _():
            copies[3].start()

    def wait_recv(copies):
        copies[0].wait_recv()
        copies[1].wait_recv()

        @pl.when(jnp.logical_not(is_bottom))
        def _():
            copies[2].wait_recv()

        @pl.when(jnp.logical_not(is_top))
        def _():
            copies[3].wait_recv()

    def wait_send(copies):
        copies[0].wait_send()
        copies[1].wait_send()

        @pl.when(jnp.logical_not(is_top))
        def _():
            copies[2].wait_send()

        @pl.when(jnp.logical_not(is_bottom))
        def _():
            copies[3].wait_send()

    def fold_copy(src, dst, sem, at):
        return pltpu.make_async_remote_copy(
            src_ref=src, dst_ref=dst, send_sem=fold_send.at[sem], recv_sem=fold_recv.at[sem],
            device_id=(at, lat), device_id_type=pl.DeviceIdType.MESH,
        )

    def others(body):
        def one(i, carry):
            body(lax.rem(lon + i, n_lon))
            return carry
        lax.fori_loop(1, n_lon, one, 0)

    def fold_start(step, buf):
        def products(k, carry):
            for l in range(2):
                face = nmb[k, l, pl.ds(last, 1), :]
                for t in range(2):
                    fq[step, k, pl.ds(2 * t + l, 1), :] = -(face * buf[t, k + 1, l, pl.ds(last, 1), :])
            return carry
        lax.fori_loop(0, levels, products, 0)
        others(lambda p: fold_copy(fq.at[step, p], fg.at[step, lon], 2 * step, p).start())
        fg[step, lon] = fq[step, lon]

    def fold_turn(step):
        some = pl.ds(0, n_lon - 1)
        fold_copy(fq.at[step, some], fg.at[step, some], 2 * step, east).wait_recv()
        fixed = lax.rem(fps[0] + lon * cols, n_lon * cols)
        tile = fixed // LANES
        block, odd = tile // 2, lax.rem(tile, 2)
        within = lax.rem(fixed, LANES)
        source = jnp.bitwise_and(within - lane, LANES - 1)
        low = lane <= within
        keep = jnp.logical_xor(low, jnp.broadcast_to(odd, lane.shape) == 1)
        row = lax.broadcasted_iota(jnp.int32, (8, LANES), 0)
        even_row = jnp.bitwise_and(row, 1) == 0
        for j in range(n_lon):
            turned = jnp.take_along_axis(fg[step, j], source, axis=1, mode="promise_in_bounds")
            fx[j] = turned
            fy[j] = jnp.where(even_row, pltpu.roll(turned, 7, 0), pltpu.roll(turned, 1, 0))
        for i in range(n_lon):
            here = lax.rem(block + n_lon - i, n_lon)
            before = lax.rem(block + 2 * n_lon - i - 1, n_lon)
            swapped = lax.rem(block + 2 * n_lon - i - 1 + odd, n_lon)
            straight = jnp.where(even_row, fx[here], fx[before])
            fo[step, i] = jnp.where(keep, straight, fy[swapped])
        others(lambda p: fold_copy(fo.at[step, p], fb.at[step, lon], 2 * step + 1, p).start())
        fb[step, lon] = fo[step, lon]

    def fold_wait(step):
        some = pl.ds(0, n_lon - 1)
        fold_copy(fo.at[step, some], fb.at[step, some], 2 * step + 1, east).wait_recv()

    def fold_wait_send(step):
        some = pl.ds(0, n_lon - 1)
        fold_copy(fq.at[step, some], fg.at[step, some], 2 * step, east).wait_send()
        fold_copy(fo.at[step, some], fb.at[step, some], 2 * step + 1, east).wait_send()

    def stencil(step, buf, store):
        def level(k):
            for r in range(row_tiles):
                rr = pl.ds(8 * r, 8)
                here = pl.ds(PAD + 8 * r, 8)
                above = pl.ds(PAD + 8 * r + 1, 8)
                below = pl.ds(PAD + 8 * r - 1, 8)
                packed_w, packed_e = recv_w[step, rr, :], recv_e[step, rr, :]
                value = [[buf[t, k + 1, l, here, :] for l in range(2)] for t in range(2)]
                next_e, next_w = [], []
                for t in range(2):
                    q = t * levels + k
                    left = [moved(x, LANES - 1) for x in value[t]]
                    right = [moved(x, 1) for x in value[t]]
                    edge_w = moved(packed_w, lax.rem(LANES - q, LANES))
                    edge_e = moved(packed_e, LANES - 1 - q)
                    next_e.append([jnp.where(at_last, left[1], left[0]), jnp.where(at_last, edge_e, left[1])])
                    next_w.append([jnp.where(at_first, edge_w, right[0]), jnp.where(at_first, right[0], right[1])])
                for l in range(2):
                    cc = slice(LANES * l, LANES * (l + 1))
                    ce, cw, cn = east_c[k, rr, cc], west_c[k, rr, cc], north_c[k, rr, cc]
                    cs = nmb[k, l, below, :]
                    cd, cu, cx = down_c[k + 1, rr, cc], down_c[k, rr, cc], diag_c[k, rr, cc]
                    if step == 0:
                        if l == 0:
                            cw = jnp.where(at_first, moved(packed_w, LANES - 2 * levels - k), cw)
                            west_c[k, rr, cc] = cw
                        cx = cx + cw + cs
                        diag_c[k, rr, cc] = cx
                    for t in range(2):
                        total = (
                            cx * value[t][l]
                            + ce * next_e[t][l]
                            - cw * next_w[t][l]
                            + cn * buf[t, k + 1, l, above, :]
                            - cs * buf[t, k + 1, l, below, :]
                            + cd * buf[t, k + 2, l, here, :]
                            + cu * buf[t, k, l, here, :]
                        )
                        store(t, k, l, r, total)

        loop_levels(levels, level)

    def store_inner(t, k, l, r, total):
        a1[t, k + 1, l, pl.ds(PAD + 8 * r, 8), :] = total

    def store_out(t, k, l, r, total):
        out[t, k, pl.ds(8 * r, 8), LANES * l : LANES * (l + 1)] = total

    copies = exchange(0, a0)
    start_exchange(copies)

    @pl.when(jnp.logical_not(is_top))
    def _():
        faces_north.start()

    @pl.when(is_top)
    def _():
        fold_start(0, a0)

    wait_recv(copies)

    @pl.when(jnp.logical_not(is_bottom))
    def _():
        faces_north.wait_recv()

    @pl.when(is_top)
    def _():
        fold_turn(0)

    stencil(0, a0, store_inner)

    @pl.when(is_top)
    def _():
        fold_wait(0)

        def add(k, carry):
            for t in range(2):
                for l in range(2):
                    at = pl.ds(last, 1)
                    a1[t, k + 1, l, at, :] = a1[t, k + 1, l, at, :] + fb[0, k, pl.ds(2 * t + l, 1), :]
            return carry
        lax.fori_loop(0, levels, add, 0)

    later = exchange(1, a1)

    @pl.when(is_top)
    def _():
        fold_start(1, a1)

    pack_columns(a1, send_w.at[1], 0, 0)
    pack_columns(a1, send_e.at[1], 1, LANES - 1)
    start_exchange(later)

    @pl.when(is_top)
    def _():
        fold_turn(1)

    wait_recv(later)
    stencil(1, a1, store_out)

    @pl.when(is_top)
    def _():
        fold_wait(1)

        def add(k, carry):
            for t in range(2):
                for l in range(2):
                    cc = slice(LANES * l, LANES * (l + 1))
                    at = pl.ds(rows - 1, 1)
                    out[t, k, at, cc] = out[t, k, at, cc] + fb[1, k, pl.ds(2 * t + l, 1), :]
            return carry
        lax.fori_loop(0, levels, add, 0)

    wait_send(copies)
    wait_send(later)

    @pl.when(jnp.logical_not(is_top))
    def _():
        faces_north.wait_send()

    @pl.when(is_top)
    def _():
        fold_wait_send(0)
        fold_wait_send(1)


def per_device(n_lon, n_lat, *args):
    _, levels, rows, cols = args[0].shape
    f32, i32 = jnp.float32, jnp.int32
    field = (levels, rows, cols)
    padded = (2, levels + 2, 2, rows + 2 * PAD, LANES)
    return pl.pallas_call(
        functools.partial(kernel, n_lon, n_lat),
        out_shape=jax.ShapeDtypeStruct(args[0].shape, f32),
        in_specs=[pl.BlockSpec(memory_space=pltpu.HBM)] * 9,
        out_specs=pl.BlockSpec(memory_space=pltpu.VMEM),
        scratch_shapes=[
            pltpu.VMEM(padded, f32),
            pltpu.VMEM(padded, f32),
            pltpu.VMEM((levels, 2, rows + 2 * PAD, LANES), f32),
            *[pltpu.VMEM(field, f32) for _ in range(4)],
            *[pltpu.VMEM((rows, cols), i32) for _ in range(3)],
            pltpu.SMEM((cols,), i32),
            *[pltpu.VMEM(field, f32) for _ in range(4)],
            pltpu.VMEM((levels + 1, rows, cols), f32),
            *[pltpu.VMEM((2, rows, LANES), f32) for _ in range(4)],
            pltpu.VMEM((2, levels, 8, LANES), f32),
            pltpu.VMEM((2, n_lon, 8, LANES), f32),
            pltpu.VMEM((n_lon, 8, LANES), f32),
            pltpu.VMEM((n_lon, 8, LANES), f32),
            pltpu.VMEM((2, n_lon, 8, LANES), f32),
            pltpu.VMEM((2, levels, 8, LANES), f32),
            pltpu.SemaphoreType.DMA((10,)),
            pltpu.SemaphoreType.DMA((9,)),
            pltpu.SemaphoreType.DMA((9,)),
            pltpu.SemaphoreType.DMA((4,)),
            pltpu.SemaphoreType.DMA((4,)),
        ],
        compiler_params=pltpu.CompilerParams(
            collective_id=0, has_side_effects=True, vmem_limit_bytes=32 * 1024 * 1024
        ),
    )(*args)


def solution(mesh):
    n_lon, n_lat = mesh.shape["lon"], mesh.shape["lat"]
    placed = (
        P(None, None, "lat", "lon"),
        P(None, "lat", "lon"),
        P(None, "lat", "lon"),
        P(None, "lat", "lon"),
        P(None, "lat", "lon"),
        P("lat", "lon"),
        P("lat", "lon"),
        P("lat", "lon"),
        P("lon"),
    )
    return jax.shard_map(
        functools.partial(per_device, n_lon, n_lat),
        mesh=mesh,
        in_specs=placed,
        out_specs=P(None, None, "lat", "lon"),
        check_vma=False,
    )
```

```python
import functools

import jax
import jax.numpy as jnp
from jax import lax
from jax.experimental import pallas as pl
from jax.experimental.pallas import tpu as pltpu
from jax.sharding import PartitionSpec as P

LANES = 128
PAD = 8
CHUNK = 4
MESH = pl.DeviceIdType.MESH


def kernel(
    n_lon, n_lat,
    ct, u_hbm, v_hbm, d_hbm, w_hbm, cm_hbm, em_hbm, nm_hbm, fp_hbm,
    out,
    a0, a1, nmb, ub, vb, db, wb, cmb, emb, nkb, fps,
    ctr, ur, vr, dr, wr,
    east_c, west_c, north_c, diag_c, down_c,
    row_n, row_s, from_s, from_n,
    col_e, col_w, from_w, from_e, next_e, next_w, next_from_w, next_from_e,
    c_sw, c_se, c_nw, c_ne,
    edge, add_w, add_e,
    fg, fq, fx, fy, f1, f2, fo, fb,
    load_sem, send_sem, recv_sem, fold_send, fold_recv,
):
    _, levels, rows, cols = ct.shape
    lon, lat = lax.axis_index("lon"), lax.axis_index("lat")
    east, west = lax.rem(lon + 1, n_lon), lax.rem(lon + n_lon - 1, n_lon)
    is_top, is_bottom = lat == n_lat - 1, lat == 0
    has_north, has_south = jnp.logical_not(is_top), jnp.logical_not(is_bottom)
    tiles = rows // 8
    first, last = PAD, PAD + rows - 1
    both = 2 * levels
    chunks = levels // CHUNK

    barrier = pltpu.get_barrier_semaphore()

    def greet(at):
        pl.semaphore_signal(barrier, inc=1, device_id=at, device_id_type=MESH)

    def others(body):
        def one(i, carry):
            body(lax.rem(lon + i, n_lon))
            return carry

        lax.fori_loop(1, n_lon, one, 0)

    @pl.when(is_top)
    def _():
        others(lambda p: greet((p, lat)))

    @pl.when(has_north)
    def _():
        greet((east, lat))
        greet((west, lat))
        greet((east, lat + 1))
        greet((west, lat + 1))
        greet((lon, lat + 1))

    @pl.when(has_south)
    def _():
        greet((east, lat - 1))
        greet((west, lat - 1))
        greet((lon, lat - 1))

    def load(src, dst, sem):
        copy = pltpu.make_async_copy(src, dst, load_sem.at[sem])
        copy.start()
        return copy

    tops = (0, 1, rows - 2, rows - 1)
    row_loads = [load(cm_hbm, cmb, 0), load(em_hbm, emb, 1), load(nm_hbm, nkb, 2)]
    for i, row in enumerate(tops):
        row_loads.append(load(ct.at[:, :, row, :], ctr.at[i], 3 + i))
    for i, row in enumerate((0, rows - 1)):
        row_loads.append(load(u_hbm.at[:, row, :], ur.at[i], 7 + i))
        row_loads.append(load(w_hbm.at[:, row, :], wr.at[i], 9 + i))
    for i, row in enumerate((0, rows - 2, rows - 1)):
        row_loads.append(load(v_hbm.at[:, row, :], vr.at[i], 11 + i))
        row_loads.append(load(d_hbm.at[:, row, :], dr.at[i], 14 + i))
    fold_load = load(fp_hbm, fps, 17)

    def chunk_loads(c):
        span = pl.ds(CHUNK * c, CHUNK)
        base = 18 + 6 * c
        pairs = [
            (
                ct.at[:, span, :, pl.ds(LANES * l, LANES)],
                a0.at[:, pl.ds(CHUNK * c + 1, CHUNK), l, pl.ds(PAD, rows), :],
            )
            for l in range(2)
        ]
        pairs += [(src.at[span], dst.at[span]) for src, dst in ((u_hbm, ub), (d_hbm, db), (v_hbm, vb), (w_hbm, wb))]
        return [pltpu.make_async_copy(src, dst, load_sem.at[base + i]) for i, (src, dst) in enumerate(pairs)]

    for c in range(chunks):
        for copy in chunk_loads(c):
            copy.start()

    block = jnp.zeros((rows, LANES), jnp.float32)
    line = jnp.zeros((1, LANES), jnp.float32)
    for buf in (a0, a1):
        for t in range(2):
            for k in (0, levels + 1):
                for l in range(2):
                    buf[t, k, l, pl.ds(PAD, rows), :] = block
    for l in range(2):
        down_c[0, :, LANES * l : LANES * (l + 1)] = block

    def clear(k, carry):
        for l in range(2):
            nmb[k, l, pl.ds(first - 1, 1), :] = line
            for t in range(2):
                a0[t, k + 1, l, pl.ds(first - 1, 1), :] = line
                a0[t, k + 1, l, pl.ds(last + 1, 1), :] = line
        return carry

    lax.fori_loop(0, levels, clear, 0)

    @pl.when(is_bottom)
    def _():
        from_s[...] = jnp.zeros_like(from_s)
        c_sw[...] = jnp.zeros_like(c_sw)
        c_se[...] = jnp.zeros_like(c_se)

    @pl.when(is_top)
    def _():
        from_n[...] = jnp.zeros_like(from_n)
        c_nw[...] = jnp.zeros_like(c_nw)
        c_ne[...] = jnp.zeros_like(c_ne)

    lane = lax.broadcasted_iota(jnp.int32, (8, LANES), 1)
    sub = lax.broadcasted_iota(jnp.int32, (8, LANES), 0)
    at_first, at_last = lane == 0, lane == LANES - 1
    row_lane = lax.broadcasted_iota(jnp.int32, (levels, LANES), 1)
    row_level = lax.broadcasted_iota(jnp.int32, (levels, LANES), 0)
    row_first, row_last = row_lane == 0, row_lane == LANES - 1

    def moved(value, by):
        return pltpu.roll(value, by, 1)

    def halves(l):
        return slice(LANES * l, LANES * (l + 1))

    for copy in row_loads:
        copy.wait()

    def bits(buf, row, count=1):
        mask = jnp.left_shift(jnp.full((levels, LANES), 2**count - 1, jnp.int32), row_level)
        return [jnp.bitwise_and(jnp.broadcast_to(buf[pl.ds(row, 1), halves(l)], mask.shape), mask) == mask for l in range(2)]

    def edge_row(i, row):
        at = 3 * i
        cell = [ctr[at, t] for t in range(2)]
        inner = [ctr[1 + i, t] for t in range(2)]
        open_e, open_n, open_c, open_d = bits(emb, row), bits(nkb, row), bits(cmb, row), bits(cmb, row, 2)
        plus, minus, north, south, diag, down = [], [], [], [], [], []
        for l in range(2):
            half, diff = 0.5 * ur[i, :, halves(l)], dr[2 * i, :, halves(l)]
            plus.append(jnp.where(open_e[l], half + diff, 0.0))
            minus.append(jnp.where(open_e[l], half - diff, 0.0))
            half = 0.5 * vr[2 * i, :, halves(l)]
            north.append(jnp.where(open_n[l], half + diff, 0.0))
            south.append(jnp.where(open_n[l], half - diff, 0.0))
            down.append(jnp.where(open_d[l], wr[i, :, halves(l)], 0.0))
        turned = [moved(x, 1) for x in minus]
        side = [jnp.where(row_first, 0.0, turned[0]), jnp.where(row_first, turned[0], turned[1])]
        if i == 1:
            open_b = bits(nkb, row - 1)
            beyond = [jnp.where(open_b[l], 0.5 * vr[1, :, halves(l)] - dr[1, :, halves(l)], 0.0) for l in range(2)]
        result = [[None, None], [None, None]]
        for l in range(2):
            up = pltpu.roll(down[l], 1, 0)
            diag = jnp.where(open_c[l], 1.0, 0.0) - plus[l] - north[l] - down[l] - up + side[l]
            if i == 1:
                diag = diag + beyond[l]
            for t in range(2):
                here = cell[t][:, halves(l)]
                left = [moved(cell[t][:, halves(m)], LANES - 1) for m in range(2)]
                right = [moved(cell[t][:, halves(m)], 1) for m in range(2)]
                to_e = jnp.where(row_last, left[1], left[0]) if l == 0 else jnp.where(row_last, 0.0, left[1])
                to_w = right[0] if l == 0 else jnp.where(row_first, right[0], right[1])
                total = diag * here + plus[l] * to_e - side[l] * to_w
                total = total + down[l] * pltpu.roll(here, levels - 1, 0) + up * pltpu.roll(here, 1, 0)
                if i == 0:
                    total = total + north[l] * inner[t][:, halves(l)]
                else:
                    total = total - beyond[l] * inner[t][:, halves(l)]
                result[t][l] = total
        return cell, result, plus, minus, north, south

    cell, result, plus, minus, north, south = edge_row(1, rows - 1)
    for l in range(2):
        for t in range(2):
            row_n[2 * t + l] = cell[t][:, halves(l)]
            row_n[4 + 2 * t + l] = result[t][l]
        row_n[8 + l] = south[l]
        row_n[10 + l] = north[l]
    row_n[12] = plus[1]
    row_n[13] = minus[1]
    cell, result, plus, minus, north, south = edge_row(0, 0)
    for l in range(2):
        for t in range(2):
            row_s[2 * t + l] = cell[t][:, halves(l)]
            row_s[4 + 2 * t + l] = result[t][l]
    row_s[8] = plus[1]

    count = 2 + jnp.where(is_top, n_lon - 3, 3) + jnp.where(is_bottom, 0, 3)
    pl.semaphore_wait(barrier, count)

    def remote(src, dst, sem, at):
        return pltpu.make_async_remote_copy(
            src_ref=src, dst_ref=dst, send_sem=send_sem.at[sem], recv_sem=recv_sem.at[sem],
            device_id=at, device_id_type=MESH,
        )

    to_north = remote(row_n.at[pl.ds(0, 13)], from_s.at[pl.ds(0, 13)], 0, (lon, lat + 1))
    to_south = remote(row_s, from_n, 1, (lon, lat - 1))
    to_east = remote(col_e, from_w, 2, (east, lat))
    to_west = remote(col_w, from_e, 3, (west, lat))
    later_east = remote(next_e, next_from_w, 4, (east, lat))
    later_west = remote(next_w, next_from_e, 5, (west, lat))
    tail = pl.ds(rows - 8, 8)
    to_ne = remote(col_e.at[tail], c_sw, 6, (east, lat + 1))
    to_nw = remote(col_w.at[tail], c_se, 7, (west, lat + 1))
    to_se = remote(col_e.at[pl.ds(0, 8)], c_nw, 8, (east, lat - 1))
    to_sw = remote(col_w.at[pl.ds(0, 8)], c_ne, 9, (west, lat - 1))

    def fold_copy(src, dst, sem, at):
        return pltpu.make_async_remote_copy(
            src_ref=src, dst_ref=dst, send_sem=fold_send.at[sem], recv_sem=fold_recv.at[sem],
            device_id=(at, lat), device_id_type=MESH,
        )

    some = pl.ds(0, n_lon - 1)
    fold_out = fold_copy(fq.at[some], fg.at[some], 0, east)
    fold_back = fold_copy(fo.at[some], fb.at[some], 1, east)

    @pl.when(has_north)
    def _():
        to_north.start()

    @pl.when(is_top)
    def _():
        def collect(k, carry):
            for i in range(14):
                fq[k, pl.ds(i, 1), :] = row_n[i, pl.ds(k, 1), :]
            return carry

        lax.fori_loop(0, levels, collect, 0)
        others(lambda p: fold_copy(fq.at[p], fg.at[lon], 0, p).start())
        fg[lon] = fq[lon]

    @pl.when(has_south)
    def _():
        to_south.start()

    col_e[...] = jnp.zeros_like(col_e)
    col_w[...] = jnp.zeros_like(col_w)

    def coefficients(c, carry):
        for copy in chunk_loads(c):
            copy.wait()
        for r in range(tiles):
            rr, pr = pl.ds(8 * r, 8), pl.ds(PAD + 8 * r, 8)
            pack_e, pack_w = col_e[rr, :], col_w[rr, :]
            for j in range(CHUNK):
                k = CHUNK * c + j
                bit = jnp.left_shift(jnp.int32(1), k)
                pair = jnp.left_shift(jnp.int32(3), k)
                minus, plus, norths, souths = [], [], [], []
                for l in range(2):
                    cc = halves(l)
                    half, diff = 0.5 * ub[k, rr, cc], db[k, rr, cc]
                    open_e = jnp.bitwise_and(emb[rr, cc], bit) != 0
                    plus.append(jnp.where(open_e, half + diff, 0.0))
                    minus.append(jnp.where(open_e, half - diff, 0.0))
                    half = 0.5 * vb[k, rr, cc]
                    open_n = jnp.bitwise_and(nkb[rr, cc], bit) != 0
                    norths.append(jnp.where(open_n, half + diff, 0.0))
                    souths.append(jnp.where(open_n, half - diff, 0.0))
                turned = [moved(x, 1) for x in minus]
                side = [jnp.where(at_first, 0.0, turned[0]), jnp.where(at_first, turned[0], turned[1])]
                for l in range(2):
                    cc = halves(l)
                    cells = cmb[rr, cc]
                    down = jnp.where(jnp.bitwise_and(cells, pair) == pair, wb[k, rr, cc], 0.0)
                    east_c[k, rr, cc] = plus[l]
                    west_c[k, rr, cc] = side[l]
                    north_c[k, rr, cc] = norths[l]
                    nmb[k, l, pr, :] = souths[l]
                    down_c[k + 1, rr, cc] = down
                    here = jnp.where(jnp.bitwise_and(cells, bit) != 0, 1.0, 0.0)
                    below = nmb[k, l, pl.ds(PAD + 8 * r - 1, 8), :]
                    diag_c[k, rr, cc] = here - plus[l] - norths[l] - down - down_c[k, rr, cc] + side[l] + below

                def put(pack, value, lane_to, lane_from):
                    return jnp.where(lane == lane_to, moved(value, lax.rem(lane_to + LANES - lane_from, LANES)), pack)

                for t in range(2):
                    pack_e = put(pack_e, a0[t, k + 1, 1, pr, :], t * levels + k, LANES - 1)
                    pack_w = put(pack_w, a0[t, k + 1, 0, pr, :], t * levels + k, 0)
                pack_e = put(pack_e, minus[1], both + k, LANES - 1)
                pack_e = put(pack_e, plus[1], 2 * both + k, LANES - 1)
                if r == tiles - 1:
                    pack_e = put(pack_e, souths[1], 3 * both + k, LANES - 1)
                    pack_w = put(pack_w, souths[0], both + k, 0)
                    pack_w = put(pack_w, norths[0], 2 * both + k, 0)
                    extra = pl.ds(rows, 8)
                    col_e[extra, :] = put(col_e[extra, :], norths[1], k, LANES - 1)
            col_e[rr, :] = pack_e
            col_w[rr, :] = pack_w
        return carry

    lax.fori_loop(0, chunks, coefficients, 0)

    def doubled(pack, starts):
        again = moved(pack, levels)
        for start in starts:
            pack = jnp.where(jnp.logical_and(lane >= start + levels, lane < start + both), again, pack)
        return pack

    for r in range(tiles):
        rr = pl.ds(8 * r, 8)
        col_e[rr, :] = doubled(col_e[rr, :], (both, 2 * both, 3 * both))
    extra = pl.ds(rows, 8)
    col_e[extra, :] = doubled(col_e[extra, :], (0,))
    col_w[tail, :] = doubled(col_w[tail, :], (both, 2 * both))

    to_east.start()
    to_west.start()

    @pl.when(has_north)
    def _():
        to_ne.start()
        to_nw.start()

    @pl.when(has_south)
    def _():
        to_se.start()
        to_sw.start()

    def first_step(c, carry):
        for r in range(tiles):
            rr, here = pl.ds(8 * r, 8), pl.ds(PAD + 8 * r, 8)
            above, below = pl.ds(PAD + 8 * r + 1, 8), pl.ds(PAD + 8 * r - 1, 8)
            for j in range(CHUNK):
                k = CHUNK * c + j
                for l in range(2):
                    cc = halves(l)
                    ce, cw, cn, cs = east_c[k, rr, cc], west_c[k, rr, cc], north_c[k, rr, cc], nmb[k, l, below, :]
                    cd, cu, cx = down_c[k + 1, rr, cc], down_c[k, rr, cc], diag_c[k, rr, cc]
                    for t in range(2):
                        value = [a0[t, k + 1, m, here, :] for m in range(2)]
                        left_1 = moved(value[1], LANES - 1)
                        right_0 = moved(value[0], 1)
                        if l == 0:
                            to_e, to_w = jnp.where(at_last, left_1, moved(value[0], LANES - 1)), right_0
                        else:
                            to_e = jnp.where(at_last, 0.0, left_1)
                            to_w = jnp.where(at_first, right_0, moved(value[1], 1))
                        total = (
                            cx * value[l]
                            + ce * to_e
                            - cw * to_w
                            + cn * a0[t, k + 1, l, above, :]
                            - cs * a0[t, k + 1, l, below, :]
                            + cd * a0[t, k + 2, l, here, :]
                            + cu * a0[t, k, l, here, :]
                        )
                        a1[t, k + 1, l, here, :] = total
        return carry

    lax.fori_loop(0, chunks, first_step, 0)

    def pack_result(c, packs):
        packs = list(packs)
        for j in range(CHUNK):
            k = CHUNK * c + j
            for t in range(2):
                q = t * levels + k
                for r in range(tiles):
                    here = pl.ds(PAD + 8 * r, 8)
                    packs[r] = jnp.where(lane == q, moved(a1[t, k + 1, 1, here, :], q + 1), packs[r])
                    packs[tiles + r] = jnp.where(lane == q, moved(a1[t, k + 1, 0, here, :], q), packs[tiles + r])
        return tuple(packs)

    packs = lax.fori_loop(0, chunks, pack_result, tuple(jnp.zeros((8, LANES), jnp.float32) for _ in range(2 * tiles)))
    for r in range(tiles):
        next_e[pl.ds(8 * r, 8), :] = packs[r]
        next_w[pl.ds(8 * r, 8), :] = packs[tiles + r]
    later_east.start()
    later_west.start()

    even = jnp.bitwise_and(sub, 1) == 0

    @pl.when(is_top)
    def _():
        fold_load.wait()
        fold_out.wait_recv()
        fixed = lax.rem(fps[0] + lon * cols, n_lon * cols)
        tile = fixed // LANES
        home, odd = tile // 2, lax.rem(tile, 2)
        within = lax.rem(fixed, LANES)
        source = jnp.bitwise_and(within - lane, LANES - 1)
        keep = jnp.logical_xor(lane <= within, jnp.broadcast_to(odd, lane.shape) == 1)

        def faces(j, at):
            shape = (8, LANES)
            return jnp.where(
                even,
                jnp.broadcast_to(fg[j, pl.ds(at, 1), :], shape),
                jnp.broadcast_to(fg[j, pl.ds(at + 1, 1), :], shape),
            )

        def turn(j, value):
            turned = jnp.take_along_axis(value, source, axis=1, mode="promise_in_bounds")
            fx[j] = turned
            fy[j] = jnp.where(even, pltpu.roll(turned, 7, 0), pltpu.roll(turned, 1, 0))

        def turned(i):
            here = lax.rem(home + n_lon - i, n_lon)
            before = lax.rem(home + 2 * n_lon - i - 1, n_lon)
            swapped = lax.rem(home + 2 * n_lon - i - 1 + odd, n_lon)
            return jnp.where(keep, jnp.where(even, fx[here], fx[before]), fy[swapped])

        for j in range(n_lon):
            turn(j, -(faces(j, 8) * fg[j, pl.ds(0, 8), :]))
        for i in range(n_lon):
            f1[i] = turned(i)
        for j in range(n_lon):
            e, w = (j + 1) % n_lon, (j - 1) % n_lon
            own = fg[j, pl.ds(0, 8), :]
            to_w = pltpu.roll(moved(fg[w, pl.ds(0, 8), :], 1), 7, 0)
            to_e = pltpu.roll(moved(fg[e, pl.ds(0, 8), :], LANES - 1), 1, 0)
            face_w = moved(jnp.broadcast_to(fg[w, pl.ds(13, 1), :], (8, LANES)), 1)
            face_e = jnp.broadcast_to(fg[j, pl.ds(12, 1), :], (8, LANES))
            inner = pltpu.roll(own, 4, 0) + f1[j]
            inner = inner + jnp.where(jnp.logical_and(even, at_first), face_w * (own - to_w), 0.0)
            inner = inner + jnp.where(jnp.logical_and(jnp.logical_not(even), at_last), face_e * to_e, 0.0)
            f2[j] = -(faces(j, 8) * inner)
        for j in range(n_lon):
            turn(j, f2[j])
        low = sub < 4
        for i in range(n_lon):
            e, w = (i + 1) % n_lon, (i - 1) % n_lon
            fo[i, pl.ds(0, 8), :] = jnp.where(low, f1[i], pltpu.roll(turned(i), 4, 0))
            fo[i, pl.ds(8, 8), :] = jnp.where(low, f1[w], pltpu.roll(f1[e], 4, 0))
        others(lambda p: fold_copy(fo.at[p], fb.at[lon], 1, p).start())
        fb[lon] = fo[lon]

    @pl.when(has_south)
    def _():
        to_north.wait_recv()
        to_ne.wait_recv()
        to_nw.wait_recv()

    @pl.when(has_north)
    def _():
        to_south.wait_recv()
        to_se.wait_recv()
        to_sw.wait_recv()

    to_east.wait_recv()
    to_west.wait_recv()
    later_east.wait_recv()
    later_west.wait_recv()

    def upright(ref, row, base):
        spread = jnp.broadcast_to(ref[pl.ds(row, 1), :], (levels, LANES))
        return jnp.sum(jnp.where(row_lane == row_level + base, spread, 0.0), axis=1, keepdims=True)

    face_sw, face_nw = upright(c_sw, 7, both), upright(c_nw, 0, both)
    for t in range(2):
        point = t * levels
        for l in range(2):
            at = 2 * t + l
            own, there = row_s[at], from_s[at]
            edge[at] = from_s[8 + l] * (own - there)
            ghost = from_s[4 + at] + from_s[10 + l] * own
            if l == 0:
                ghost = ghost + jnp.where(row_first, face_sw * (there - upright(c_sw, 7, point)), 0.0)
            else:
                ghost = ghost + jnp.where(row_last, from_s[12] * upright(c_se, 7, point), 0.0)
            edge[8 + at] = ghost
            own, there = row_n[at], from_n[at]
            edge[4 + at] = row_n[10 + l] * there
            ghost = from_n[4 + at] + row_n[8 + l] * (there - own)
            if l == 0:
                ghost = ghost + jnp.where(row_first, face_nw * (there - upright(c_nw, 0, point)), 0.0)
            else:
                ghost = ghost + jnp.where(row_last, from_n[8] * upright(c_ne, 0, point), 0.0)
            edge[12 + at] = jnp.where(is_top, 0.0, ghost)

    for r in range(tiles):
        rr = pl.ds(8 * r, 8)
        got = from_w[rr, :]
        own = col_w[rr, :]
        face = moved(got, LANES - both)
        ghost = next_from_w[rr, :] + moved(got, LANES - 2 * both) * own
        if r == 0:
            corner = c_sw[...]
            beyond = pltpu.roll(moved(corner, LANES - 3 * both), 1, 0)
            ghost = ghost + jnp.where(sub == 0, beyond * (got - pltpu.roll(corner, 1, 0)), 0.0)
        if r == tiles - 1:
            ghost = ghost + jnp.where(sub == 7, from_w[extra, :] * pltpu.roll(c_nw[...], 7, 0), 0.0)
        next_from_w[rr, :] = ghost
        add_w[rr, :] = face * (own - got)
        got = from_e[rr, :]
        mine = col_e[rr, :]
        ghost = next_from_e[rr, :] + moved(mine, LANES - both) * (got - mine)
        if r == 0:
            corner = c_se[...]
            beyond = pltpu.roll(moved(corner, LANES - both), 1, 0)
            ghost = ghost + jnp.where(sub == 0, beyond * (got - pltpu.roll(corner, 1, 0)), 0.0)
        if r == tiles - 1:
            ghost = ghost + jnp.where(sub == 7, moved(got, LANES - 2 * both) * pltpu.roll(c_ne[...], 7, 0), 0.0)
        next_from_e[rr, :] = ghost
        add_e[rr, :] = moved(mine, LANES - 2 * both) * got

    @pl.when(is_top)
    def _():
        fold_back.wait_recv()

        def ghosts(k, carry):
            rr = pl.ds(rows - 8, 8)
            ghost_w, ghost_e = next_from_w[rr, :], next_from_e[rr, :]
            for t in range(2):
                at = jnp.logical_and(sub == 7, lane == t * levels + k)
                value = jnp.broadcast_to(fb[k, pl.ds(8 + 2 * t + 1, 1), :], (8, LANES))
                ghost_w = ghost_w + jnp.where(at, moved(value, t * levels + k + 1), 0.0)
                value = jnp.broadcast_to(fb[k, pl.ds(12 + 2 * t, 1), :], (8, LANES))
                ghost_e = ghost_e + jnp.where(at, moved(value, t * levels + k), 0.0)
            next_from_w[rr, :] = ghost_w
            next_from_e[rr, :] = ghost_e
            for t in range(2):
                for l in range(2):
                    at = pl.ds(last, 1)
                    a1[t, k + 1, l, at, :] = a1[t, k + 1, l, at, :] + fb[k, pl.ds(2 * t + l, 1), :]
            return carry

        lax.fori_loop(0, levels, ghosts, 0)

    def complete(c, carry):
        for j in range(CHUNK):
            k = CHUNK * c + j
            at = pl.ds(k, 1)
            for l in range(2):
                nmb[k, l, pl.ds(first - 1, 1), :] = from_s[8 + l, at, :]
                for t in range(2):
                    i = 2 * t + l
                    low, high = pl.ds(first, 1), pl.ds(last, 1)
                    a1[t, k + 1, l, low, :] = a1[t, k + 1, l, low, :] + edge[i, at, :]
                    a1[t, k + 1, l, high, :] = a1[t, k + 1, l, high, :] + edge[4 + i, at, :]
                    a1[t, k + 1, l, pl.ds(first - 1, 1), :] = edge[8 + i, at, :]
                    a1[t, k + 1, l, pl.ds(last + 1, 1), :] = edge[12 + i, at, :]
            for r in range(tiles):
                rr, here = pl.ds(8 * r, 8), pl.ds(PAD + 8 * r, 8)
                for t in range(2):
                    q = t * levels + k
                    value = moved(add_w[rr, :], lax.rem(LANES - q, LANES))
                    a1[t, k + 1, 0, here, :] = a1[t, k + 1, 0, here, :] + jnp.where(at_first, value, 0.0)
                    value = moved(add_e[rr, :], LANES - 1 - q)
                    a1[t, k + 1, 1, here, :] = a1[t, k + 1, 1, here, :] + jnp.where(at_last, value, 0.0)
        return carry

    lax.fori_loop(0, chunks, complete, 0)

    def second_step(c, carry):
        for r in range(tiles):
            rr, here = pl.ds(8 * r, 8), pl.ds(PAD + 8 * r, 8)
            above, below = pl.ds(PAD + 8 * r + 1, 8), pl.ds(PAD + 8 * r - 1, 8)
            ghost_w, ghost_e, face_w = next_from_w[rr, :], next_from_e[rr, :], from_w[rr, :]
            for j in range(CHUNK):
                k = CHUNK * c + j
                for l in range(2):
                    cc = halves(l)
                    ce, cw, cn, cs = east_c[k, rr, cc], west_c[k, rr, cc], north_c[k, rr, cc], nmb[k, l, below, :]
                    cd, cu, cx = down_c[k + 1, rr, cc], down_c[k, rr, cc], diag_c[k, rr, cc]
                    if l == 0:
                        face = jnp.where(at_first, moved(face_w, LANES - both - k), 0.0)
                        cw, cx = cw + face, cx + face
                    if r == 0:
                        cx = cx + jnp.where(sub == 0, cs, 0.0)
                    for t in range(2):
                        q = t * levels + k
                        value = [a1[t, k + 1, m, here, :] for m in range(2)]
                        left_1 = moved(value[1], LANES - 1)
                        right_0 = moved(value[0], 1)
                        if l == 0:
                            to_e = jnp.where(at_last, left_1, moved(value[0], LANES - 1))
                            to_w = jnp.where(at_first, moved(ghost_w, lax.rem(LANES - q, LANES)), right_0)
                        else:
                            to_e = jnp.where(at_last, moved(ghost_e, LANES - 1 - q), left_1)
                            to_w = jnp.where(at_first, right_0, moved(value[1], 1))
                        total = (
                            cx * value[l]
                            + ce * to_e
                            - cw * to_w
                            + cn * a1[t, k + 1, l, above, :]
                            - cs * a1[t, k + 1, l, below, :]
                            + cd * a1[t, k + 2, l, here, :]
                            + cu * a1[t, k, l, here, :]
                        )
                        out[t, k, rr, cc] = total
        return carry

    lax.fori_loop(0, chunks, second_step, 0)

    @pl.when(is_top)
    def _():
        def add(k, carry):
            for t in range(2):
                for l in range(2):
                    at = pl.ds(rows - 1, 1)
                    out[t, k, at, halves(l)] = out[t, k, at, halves(l)] + fb[k, pl.ds(4 + 2 * t + l, 1), :]
            return carry

        lax.fori_loop(0, levels, add, 0)

    to_east.wait_send()
    to_west.wait_send()
    later_east.wait_send()
    later_west.wait_send()

    @pl.when(has_north)
    def _():
        to_north.wait_send()
        to_ne.wait_send()
        to_nw.wait_send()
        fold_load.wait()

    @pl.when(has_south)
    def _():
        to_south.wait_send()
        to_se.wait_send()
        to_sw.wait_send()

    @pl.when(is_top)
    def _():
        fold_out.wait_send()
        fold_back.wait_send()


def per_device(n_lon, n_lat, *args):
    _, levels, rows, cols = args[0].shape
    f32, i32 = jnp.float32, jnp.int32
    field = (levels, rows, cols)
    padded = (2, levels + 2, 2, rows + 2 * PAD, LANES)
    args = [pltpu.with_memory_space_constraint(value, pltpu.HBM) for value in args]
    column = (rows, LANES)
    return pl.pallas_call(
        functools.partial(kernel, n_lon, n_lat),
        out_shape=jax.ShapeDtypeStruct(args[0].shape, f32),
        in_specs=[pl.BlockSpec(memory_space=pltpu.HBM)] * 9,
        out_specs=pl.BlockSpec(memory_space=pltpu.VMEM),
        scratch_shapes=[
            pltpu.VMEM(padded, f32),
            pltpu.VMEM(padded, f32),
            pltpu.VMEM((levels, 2, rows + 2 * PAD, LANES), f32),
            *[pltpu.VMEM(field, f32) for _ in range(4)],
            *[pltpu.VMEM((rows, cols), i32) for _ in range(3)],
            pltpu.SMEM((cols,), i32),
            pltpu.VMEM((4, 2, levels, cols), f32),
            pltpu.VMEM((2, levels, cols), f32),
            pltpu.VMEM((3, levels, cols), f32),
            pltpu.VMEM((3, levels, cols), f32),
            pltpu.VMEM((2, levels, cols), f32),
            *[pltpu.VMEM(field, f32) for _ in range(4)],
            pltpu.VMEM((levels + 1, rows, cols), f32),
            pltpu.VMEM((14, levels, LANES), f32),
            pltpu.VMEM((9, levels, LANES), f32),
            pltpu.VMEM((14, levels, LANES), f32),
            pltpu.VMEM((9, levels, LANES), f32),
            pltpu.VMEM((rows + 8, LANES), f32),
            pltpu.VMEM(column, f32),
            pltpu.VMEM((rows + 8, LANES), f32),
            *[pltpu.VMEM(column, f32) for _ in range(5)],
            *[pltpu.VMEM((8, LANES), f32) for _ in range(4)],
            pltpu.VMEM((16, levels, LANES), f32),
            pltpu.VMEM(column, f32),
            pltpu.VMEM(column, f32),
            pltpu.VMEM((n_lon, 16, LANES), f32),
            pltpu.VMEM((n_lon, 16, LANES), f32),
            *[pltpu.VMEM((n_lon, 8, LANES), f32) for _ in range(4)],
            pltpu.VMEM((n_lon, 16, LANES), f32),
            pltpu.VMEM((n_lon, 16, LANES), f32),
            pltpu.SemaphoreType.DMA((18 + 6 * (levels // CHUNK),)),
            pltpu.SemaphoreType.DMA((10,)),
            pltpu.SemaphoreType.DMA((10,)),
            pltpu.SemaphoreType.DMA((2,)),
            pltpu.SemaphoreType.DMA((2,)),
        ],
        compiler_params=pltpu.CompilerParams(
            collective_id=0, has_side_effects=True, vmem_limit_bytes=32 * 1024 * 1024
        ),
    )(*args)


def solution(mesh):
    n_lon, n_lat = mesh.shape["lon"], mesh.shape["lat"]
    placed = (
        P(None, None, "lat", "lon"),
        P(None, "lat", "lon"),
        P(None, "lat", "lon"),
        P(None, "lat", "lon"),
        P(None, "lat", "lon"),
        P("lat", "lon"),
        P("lat", "lon"),
        P("lat", "lon"),
        P("lon"),
    )
    return jax.shard_map(
        functools.partial(per_device, n_lon, n_lat),
        mesh=mesh,
        in_specs=placed,
        out_specs=P(None, None, "lat", "lon"),
        check_vma=False,
    )
```

```python
import functools

import jax
import jax.numpy as jnp
from jax import lax
from jax.experimental import pallas as pl
from jax.experimental.pallas import tpu as pltpu
from jax.sharding import PartitionSpec as P

LANES = 128
PAD = 8
CHUNK = 4
MESH = pl.DeviceIdType.MESH


def kernel(
    n_lon, n_lat,
    ct, u_hbm, v_hbm, d_hbm, w_hbm, cm_hbm, em_hbm, nm_hbm, fp_hbm,
    out,
    a0, a1, nmb, ub, vb, db, wb, cmb, emb, nkb, fps,
    ctr, ur, vr, dr, wr,
    east_c, west_c, north_c, diag_c, down_c,
    row_n, row_s, from_s, from_n,
    col_e, col_w, from_w, from_e, next_e, next_w, next_from_w, next_from_e,
    tiles_out, tiles_in, tiles_w, tiles_e,
    edge, last_c, add_w, add_e,
    fg, fq, fx, fy, gx, gy, f1, f2, fo, fb,
    load_sem, send_sem, recv_sem, fold_send, fold_recv,
):
    _, levels, rows, cols = ct.shape
    lon, lat = lax.axis_index("lon"), lax.axis_index("lat")
    east, west = lax.rem(lon + 1, n_lon), lax.rem(lon + n_lon - 1, n_lon)
    is_top, is_bottom = lat == n_lat - 1, lat == 0
    has_north, has_south = jnp.logical_not(is_top), jnp.logical_not(is_bottom)
    tiles = rows // 8
    first, last = PAD, PAD + rows - 1
    both = 2 * levels
    chunks = levels // CHUNK

    barrier = pltpu.get_barrier_semaphore()

    def greet(at):
        pl.semaphore_signal(barrier, inc=1, device_id=at, device_id_type=MESH)

    def others(body):
        def one(i, carry):
            body(lax.rem(lon + i, n_lon))
            return carry

        lax.fori_loop(1, n_lon, one, 0)

    @pl.when(is_top)
    def _():
        others(lambda p: greet((p, lat)))

    @pl.when(has_north)
    def _():
        greet((east, lat))
        greet((west, lat))
        greet((lon, lat + 1))

    @pl.when(has_south)
    def _():
        greet((lon, lat - 1))

    def load(src, dst, sem):
        copy = pltpu.make_async_copy(src, dst, load_sem.at[sem])
        copy.start()
        return copy

    tops = (0, 1, rows - 2, rows - 1)
    row_loads = [load(cm_hbm, cmb, 0), load(em_hbm, emb, 1), load(nm_hbm, nkb, 2)]
    for i, row in enumerate(tops):
        row_loads.append(load(ct.at[:, :, row, :], ctr.at[i], 3 + i))
    for i, row in enumerate((0, rows - 1)):
        row_loads.append(load(u_hbm.at[:, row, :], ur.at[i], 7 + i))
        row_loads.append(load(w_hbm.at[:, row, :], wr.at[i], 9 + i))
    for i, row in enumerate((0, rows - 2, rows - 1)):
        row_loads.append(load(v_hbm.at[:, row, :], vr.at[i], 11 + i))
        row_loads.append(load(d_hbm.at[:, row, :], dr.at[i], 14 + i))
    fold_load = load(fp_hbm, fps, 17)

    def chunk_loads(c):
        span = pl.ds(CHUNK * c, CHUNK)
        base = 18 + 6 * c
        pairs = [
            (
                ct.at[:, span, :, pl.ds(LANES * l, LANES)],
                a0.at[:, pl.ds(CHUNK * c + 1, CHUNK), l, pl.ds(PAD, rows), :],
            )
            for l in range(2)
        ]
        pairs += [(src.at[span], dst.at[span]) for src, dst in ((u_hbm, ub), (d_hbm, db), (v_hbm, vb), (w_hbm, wb))]
        return [pltpu.make_async_copy(src, dst, load_sem.at[base + i]) for i, (src, dst) in enumerate(pairs)]

    for c in range(chunks):
        for copy in chunk_loads(c):
            copy.start()

    block = jnp.zeros((rows, LANES), jnp.float32)
    line = jnp.zeros((1, LANES), jnp.float32)
    for buf in (a0, a1):
        for t in range(2):
            for k in (0, levels + 1):
                for l in range(2):
                    buf[t, k, l, pl.ds(PAD, rows), :] = block
    for l in range(2):
        down_c[0, :, LANES * l : LANES * (l + 1)] = block

    def clear(k, carry):
        for l in range(2):
            nmb[k, l, pl.ds(first - 1, 1), :] = line
            for t in range(2):
                a0[t, k + 1, l, pl.ds(first - 1, 1), :] = line
                a0[t, k + 1, l, pl.ds(last + 1, 1), :] = line
        return carry

    lax.fori_loop(0, levels, clear, 0)

    @pl.when(is_bottom)
    def _():
        from_s[...] = jnp.zeros_like(from_s)
        tiles_in[0] = jnp.zeros((levels, LANES), jnp.float32)

    @pl.when(is_top)
    def _():
        from_n[...] = jnp.zeros_like(from_n)
        tiles_in[1] = jnp.zeros((levels, LANES), jnp.float32)

    lane = lax.broadcasted_iota(jnp.int32, (8, LANES), 1)
    sub = lax.broadcasted_iota(jnp.int32, (8, LANES), 0)
    at_first, at_last = lane == 0, lane == LANES - 1
    row_lane = lax.broadcasted_iota(jnp.int32, (levels, LANES), 1)
    row_level = lax.broadcasted_iota(jnp.int32, (levels, LANES), 0)
    row_first, row_last = row_lane == 0, row_lane == LANES - 1

    def moved(value, by):
        return pltpu.roll(value, by, 1)

    def halves(l):
        return slice(LANES * l, LANES * (l + 1))

    for copy in row_loads:
        copy.wait()

    def bits(buf, row, count=1):
        mask = jnp.left_shift(jnp.full((levels, LANES), 2**count - 1, jnp.int32), row_level)
        return [jnp.bitwise_and(jnp.broadcast_to(buf[pl.ds(row, 1), halves(l)], mask.shape), mask) == mask for l in range(2)]

    def edge_row(i, row):
        at = 3 * i
        cell = [ctr[at, t] for t in range(2)]
        inner = [ctr[1 + i, t] for t in range(2)]
        open_e, open_n, open_c, open_d = bits(emb, row), bits(nkb, row), bits(cmb, row), bits(cmb, row, 2)
        plus, minus, north, south, diag, down = [], [], [], [], [], []
        for l in range(2):
            half, diff = 0.5 * ur[i, :, halves(l)], dr[2 * i, :, halves(l)]
            plus.append(jnp.where(open_e[l], half + diff, 0.0))
            minus.append(jnp.where(open_e[l], half - diff, 0.0))
            half = 0.5 * vr[2 * i, :, halves(l)]
            north.append(jnp.where(open_n[l], half + diff, 0.0))
            south.append(jnp.where(open_n[l], half - diff, 0.0))
            down.append(jnp.where(open_d[l], wr[i, :, halves(l)], 0.0))
        turned = [moved(x, 1) for x in minus]
        side = [jnp.where(row_first, 0.0, turned[0]), jnp.where(row_first, turned[0], turned[1])]
        if i == 1:
            open_b = bits(nkb, row - 1)
            beyond = [jnp.where(open_b[l], 0.5 * vr[1, :, halves(l)] - dr[1, :, halves(l)], 0.0) for l in range(2)]
        result = [[None, None], [None, None]]
        for l in range(2):
            up = pltpu.roll(down[l], 1, 0)
            diag = jnp.where(open_c[l], 1.0, 0.0) - plus[l] - north[l] - down[l] - up + side[l]
            if i == 1:
                diag = diag + beyond[l]
                last_c[l], last_c[2 + l], last_c[4 + l], last_c[6 + l] = diag, plus[l], side[l], down[l]
                last_c[8 + l] = jnp.where(open_b[l], 0.5 * vr[1, :, halves(l)] + dr[1, :, halves(l)], 0.0)
            for t in range(2):
                here = cell[t][:, halves(l)]
                left = [moved(cell[t][:, halves(m)], LANES - 1) for m in range(2)]
                right = [moved(cell[t][:, halves(m)], 1) for m in range(2)]
                to_e = jnp.where(row_last, left[1], left[0]) if l == 0 else jnp.where(row_last, 0.0, left[1])
                to_w = right[0] if l == 0 else jnp.where(row_first, right[0], right[1])
                total = diag * here + plus[l] * to_e - side[l] * to_w
                total = total + down[l] * pltpu.roll(here, levels - 1, 0) + up * pltpu.roll(here, 1, 0)
                if i == 0:
                    total = total + north[l] * inner[t][:, halves(l)]
                else:
                    total = total - beyond[l] * inner[t][:, halves(l)]
                result[t][l] = total
        return cell, result, plus, minus, north, south

    cell, result, plus, minus, north, south = edge_row(1, rows - 1)
    for l in range(2):
        for t in range(2):
            row_n[2 * t + l] = cell[t][:, halves(l)]
            row_n[4 + 2 * t + l] = result[t][l]
        row_n[8 + l] = south[l]
        row_n[12 + l] = north[l]
    row_n[10] = plus[1]
    row_n[11] = minus[1]

    def corner_tile(cell, minus, plus, south):
        tile = jnp.zeros((levels, LANES), jnp.float32)
        for to, value, at in (
            (0, cell[0][:, halves(0)], 0), (1, cell[1][:, halves(0)], 0), (2, south[0], 0),
            (8, cell[0][:, halves(1)], LANES - 1), (9, cell[1][:, halves(1)], LANES - 1), (10, south[1], LANES - 1),
            (11, minus[1], LANES - 1), (12, plus[1], LANES - 1),
        ):
            tile = jnp.where(row_lane == to, moved(value, (to - at) % LANES), tile)
        return tile

    tiles_out[0] = corner_tile(cell, minus, plus, south)
    cell, result, plus, minus, north, south = edge_row(0, 0)
    for l in range(2):
        for t in range(2):
            row_s[2 * t + l] = cell[t][:, halves(l)]
            row_s[4 + 2 * t + l] = result[t][l]
    row_s[8] = plus[1]
    tiles_out[1] = corner_tile(cell, minus, plus, south)

    def remote(src, dst, sem, at):
        return pltpu.make_async_remote_copy(
            src_ref=src, dst_ref=dst, send_sem=send_sem.at[sem], recv_sem=recv_sem.at[sem],
            device_id=at, device_id_type=MESH,
        )

    to_north = remote(row_n.at[pl.ds(0, 10)], from_s.at[pl.ds(0, 10)], 0, (lon, lat + 1))
    to_north_too = remote(row_n.at[pl.ds(12, 2)], from_s.at[pl.ds(12, 2)], 10, (lon, lat + 1))
    to_south = remote(row_s.at[pl.ds(0, 8)], from_n.at[pl.ds(0, 8)], 1, (lon, lat - 1))
    to_east = remote(col_e, from_w, 2, (east, lat))
    to_west = remote(col_w, from_e, 3, (west, lat))
    later_east = remote(next_e, next_from_w, 4, (east, lat))
    later_west = remote(next_w, next_from_e, 5, (west, lat))
    tail = pl.ds(rows - 8, 8)
    tile_north = remote(tiles_out.at[0], tiles_in.at[0], 6, (lon, lat + 1))
    tile_south = remote(tiles_out.at[1], tiles_in.at[1], 7, (lon, lat - 1))
    relay_east = remote(tiles_in, tiles_w, 8, (east, lat))
    relay_west = remote(tiles_in, tiles_e, 9, (west, lat))

    def fold_copy(src, dst, sem, at):
        return pltpu.make_async_remote_copy(
            src_ref=src, dst_ref=dst, send_sem=fold_send.at[sem], recv_sem=fold_recv.at[sem],
            device_id=(at, lat), device_id_type=MESH,
        )

    some = pl.ds(0, n_lon - 1)
    fold_out = fold_copy(fq.at[some, pl.ds(0, 12)], fg.at[some, pl.ds(0, 12)], 0, east)
    fold_back = fold_copy(fo.at[some, pl.ds(0, 11)], fb.at[:, some, :], 1, east)

    def first_sends():
        count = 2 + jnp.where(is_top, n_lon - 3, 1) + jnp.where(is_bottom, 0, 1)
        pl.semaphore_wait(barrier, count)

        @pl.when(is_top)
        def _():
            others(lambda p: fold_copy(fq.at[p, pl.ds(0, 12)], fg.at[lon, pl.ds(0, 12)], 0, p).start())
            fg[lon] = fq[lon]

        @pl.when(has_north)
        def _():
            tile_north.start()
            to_north.start()
            to_north_too.start()

        @pl.when(has_south)
        def _():
            tile_south.start()
            to_south.start()

    @pl.when(is_top)
    def _():
        def collect(k, carry):
            for i in range(12):
                fq[k, pl.ds(i, 1), :] = row_n[i, pl.ds(k, 1), :]
            return carry

        lax.fori_loop(0, levels, collect, 0)

    x, y = lax.rem(lon, 4), lax.rem(lat, 4)
    ahead = jnp.logical_or(
        jnp.logical_or(jnp.logical_and(y == 0, x <= 1), y == 1),
        jnp.logical_or(jnp.logical_and(y == 2, x == 3), jnp.logical_and(y == 3, x >= 2)),
    )
    ahead = jnp.logical_or(ahead, jnp.logical_and(lat == 0, lon == n_lon - 1))
    ahead = jnp.logical_and(ahead, jnp.logical_or(lon > 0, lat > 0))

    @pl.when(jnp.logical_not(ahead))
    def _():
        first_sends()

    col_e[...] = jnp.zeros_like(col_e)
    col_w[...] = jnp.zeros_like(col_w)

    def coefficients(c, carry):
        for copy in chunk_loads(c):
            copy.wait()
        for r in range(tiles):
            rr, pr = pl.ds(8 * r, 8), pl.ds(PAD + 8 * r, 8)
            pack_e, pack_w = col_e[rr, :], col_w[rr, :]
            for j in range(CHUNK):
                k = CHUNK * c + j
                bit = jnp.left_shift(jnp.int32(1), k)
                pair = jnp.left_shift(jnp.int32(3), k)
                minus, plus, norths, souths = [], [], [], []
                for l in range(2):
                    cc = halves(l)
                    half, diff = 0.5 * ub[k, rr, cc], db[k, rr, cc]
                    open_e = jnp.bitwise_and(emb[rr, cc], bit) != 0
                    plus.append(jnp.where(open_e, half + diff, 0.0))
                    minus.append(jnp.where(open_e, half - diff, 0.0))
                    half = 0.5 * vb[k, rr, cc]
                    open_n = jnp.bitwise_and(nkb[rr, cc], bit) != 0
                    norths.append(jnp.where(open_n, half + diff, 0.0))
                    souths.append(jnp.where(open_n, half - diff, 0.0))
                turned = [moved(x, 1) for x in minus]
                side = [jnp.where(at_first, 0.0, turned[0]), jnp.where(at_first, turned[0], turned[1])]
                for l in range(2):
                    cc = halves(l)
                    cells = cmb[rr, cc]
                    down = jnp.where(jnp.bitwise_and(cells, pair) == pair, wb[k, rr, cc], 0.0)
                    east_c[k, rr, cc] = plus[l]
                    west_c[k, rr, cc] = side[l]
                    north_c[k, rr, cc] = norths[l]
                    nmb[k, l, pr, :] = souths[l]
                    down_c[k + 1, rr, cc] = down
                    here = jnp.where(jnp.bitwise_and(cells, bit) != 0, 1.0, 0.0)
                    below = nmb[k, l, pl.ds(PAD + 8 * r - 1, 8), :]
                    diag_c[k, rr, cc] = here - plus[l] - norths[l] - down - down_c[k, rr, cc] + side[l] + below

                def put(pack, value, lane_to, lane_from):
                    return jnp.where(lane == lane_to, moved(value, lax.rem(lane_to + LANES - lane_from, LANES)), pack)

                for t in range(2):
                    pack_e = put(pack_e, a0[t, k + 1, 1, pr, :], t * levels + k, LANES - 1)
                    pack_w = put(pack_w, a0[t, k + 1, 0, pr, :], t * levels + k, 0)
                pack_e = put(pack_e, minus[1], both + k, LANES - 1)
                pack_e = put(pack_e, plus[1], 2 * both + k, LANES - 1)
                if r == tiles - 1:
                    pack_e = put(pack_e, souths[1], 3 * both + k, LANES - 1)
                    pack_w = put(pack_w, souths[0], both + k, 0)
                    pack_w = put(pack_w, norths[0], 2 * both + k, 0)
                    extra = pl.ds(rows, 8)
                    col_e[extra, :] = put(col_e[extra, :], norths[1], k, LANES - 1)
            col_e[rr, :] = pack_e
            col_w[rr, :] = pack_w
        return carry

    lax.fori_loop(0, chunks, coefficients, 0)

    def doubled(pack, starts):
        again = moved(pack, levels)
        for start in starts:
            pack = jnp.where(jnp.logical_and(lane >= start + levels, lane < start + both), again, pack)
        return pack

    for r in range(tiles):
        rr = pl.ds(8 * r, 8)
        col_e[rr, :] = doubled(col_e[rr, :], (both, 2 * both, 3 * both))
    extra = pl.ds(rows, 8)
    col_e[extra, :] = doubled(col_e[extra, :], (0,))
    col_w[tail, :] = doubled(col_w[tail, :], (both, 2 * both))

    def column_sends():
        to_east.start()
        to_west.start()

    @pl.when(jnp.logical_not(ahead))
    def _():
        column_sends()

    def step_levels(c, buf, second):
        for r in range(tiles):
            rr, here = pl.ds(8 * r, 8), pl.ds(PAD + 8 * r, 8)
            above, below = pl.ds(PAD + 8 * r + 1, 8), pl.ds(PAD + 8 * r - 1, 8)
            column = [
                [[buf[t, CHUNK * c + j, l, here, :] for j in range(CHUNK + 2)] for l in range(2)] for t in range(2)
            ]
            downs = [[down_c[CHUNK * c + j, rr, halves(l)] for j in range(CHUNK + 1)] for l in range(2)]
            if second:
                ghost_w, ghost_e, face_w = next_from_w[rr, :], next_from_e[rr, :], from_w[rr, :]
            for j in range(CHUNK):
                k = CHUNK * c + j
                to_e, to_w = [], []
                for t in range(2):
                    q = t * levels + k
                    value = [column[t][l][j + 1] for l in range(2)]
                    left = [moved(x, LANES - 1) for x in value]
                    right = [moved(x, 1) for x in value]
                    edge_e = moved(ghost_e, LANES - 1 - q) if second else 0.0
                    to_e.append([jnp.where(at_last, left[1], left[0]), jnp.where(at_last, edge_e, left[1])])
                    edge_w = jnp.where(at_first, moved(ghost_w, lax.rem(LANES - q, LANES)), right[0]) if second else right[0]
                    to_w.append([edge_w, jnp.where(at_first, right[0], right[1])])
                for l in range(2):
                    cc = halves(l)
                    ce, cw, cn, cs = east_c[k, rr, cc], west_c[k, rr, cc], north_c[k, rr, cc], nmb[k, l, below, :]
                    cx = diag_c[k, rr, cc]
                    if second and l == 0:
                        face = jnp.where(at_first, moved(face_w, LANES - both - k), 0.0)
                        cw, cx = cw + face, cx + face
                    if second and r == 0:
                        cx = cx + jnp.where(sub == 0, cs, 0.0)
                    for t in range(2):
                        total = cx * column[t][l][j + 1] + ce * to_e[t][l] - cw * to_w[t][l]
                        total = total + (cn * buf[t, k + 1, l, above, :] - cs * buf[t, k + 1, l, below, :])
                        total = total + (downs[l][j + 1] * column[t][l][j + 2] + downs[l][j] * column[t][l][j])
                        if second:
                            out[t, k, rr, cc] = total
                        else:
                            a1[t, k + 1, l, here, :] = total

    def first_step(c, carry):
        step_levels(c, a0, False)
        return carry

    lax.fori_loop(0, chunks, first_step, 0)

    def pack_result(c, packs):
        packs = list(packs)
        for j in range(CHUNK):
            k = CHUNK * c + j
            for t in range(2):
                q = t * levels + k
                for r in range(tiles):
                    here = pl.ds(PAD + 8 * r, 8)
                    packs[r] = jnp.where(lane == q, moved(a1[t, k + 1, 1, here, :], q + 1), packs[r])
                    packs[tiles + r] = jnp.where(lane == q, moved(a1[t, k + 1, 0, here, :], q), packs[tiles + r])
        return tuple(packs)

    packs = lax.fori_loop(0, chunks, pack_result, tuple(jnp.zeros((8, LANES), jnp.float32) for _ in range(2 * tiles)))
    for r in range(tiles):
        next_e[pl.ds(8 * r, 8), :] = packs[r]
        next_w[pl.ds(8 * r, 8), :] = packs[tiles + r]
    @pl.when(ahead)
    def _():
        first_sends()
        column_sends()

    later_east.start()
    later_west.start()

    @pl.when(has_south)
    def _():
        tile_north.wait_recv()

    @pl.when(has_north)
    def _():
        tile_south.wait_recv()

    relay_east.start()
    relay_west.start()

    even = jnp.bitwise_and(sub, 1) == 0

    @pl.when(is_top)
    def _():
        fold_load.wait()
        fold_out.wait_recv()
        fixed = lax.rem(fps[0] + lon * cols, n_lon * cols)
        tile = fixed // LANES
        home, odd = tile // 2, lax.rem(tile, 2)
        within = lax.rem(fixed, LANES)
        source = jnp.bitwise_and(within - lane, LANES - 1)
        keep = jnp.logical_xor(lane <= within, jnp.broadcast_to(odd, lane.shape) == 1)

        def faces(j, at):
            shape = (8, LANES)
            return jnp.where(
                even,
                jnp.broadcast_to(fg[j, pl.ds(at, 1), :], shape),
                jnp.broadcast_to(fg[j, pl.ds(at + 1, 1), :], shape),
            )

        def turn(j, value, straight, swapped):
            turned = jnp.take_along_axis(value, source, axis=1, mode="promise_in_bounds")
            straight[j] = turned
            swapped[j] = jnp.where(even, pltpu.roll(turned, 7, 0), pltpu.roll(turned, 1, 0))

        def turned(i, straight, swapped):
            here = lax.rem(home + n_lon - i, n_lon)
            before = lax.rem(home + 2 * n_lon - i - 1, n_lon)
            third = lax.rem(home + 2 * n_lon - i - 1 + odd, n_lon)
            return jnp.where(keep, jnp.where(even, straight[here], straight[before]), swapped[third])

        low = sub < 4
        for j in range(n_lon):
            e, w = (j + 1) % n_lon, (j - 1) % n_lon
            own = fg[j, pl.ds(0, 8), :]
            face = faces(j, 8)
            to_w = pltpu.roll(moved(fg[w, pl.ds(0, 8), :], 1), 7, 0)
            to_e = pltpu.roll(moved(fg[e, pl.ds(0, 8), :], LANES - 1), 1, 0)
            face_w = moved(jnp.broadcast_to(fg[w, pl.ds(11, 1), :], (8, LANES)), 1)
            face_e = jnp.broadcast_to(fg[j, pl.ds(10, 1), :], (8, LANES))
            inner = jnp.where(jnp.logical_and(even, at_first), face_w * (own - to_w), 0.0)
            inner = inner + jnp.where(jnp.logical_and(jnp.logical_not(even), at_last), face_e * to_e, 0.0)
            value = -(face * jnp.where(low, own, own + pltpu.roll(inner, 4, 0)))
            f2[j] = value
            turn(j, value, fx, fy)
            turn(j, face, gx, gy)
        for i in range(n_lon):
            value = turned(i, fx, fy)
            f1[i] = value
            later = value - turned(i, gx, gy) * pltpu.roll(f2[i], 4, 0)
            fo[i, pl.ds(0, 8), :] = jnp.where(low, value, later)
        for i in range(n_lon):
            e, w = (i + 1) % n_lon, (i - 1) % n_lon
            fo[i, pl.ds(8, 8), :] = jnp.where(at_last, pltpu.roll(f1[w], 7, 0), f1[e])
        others(lambda p: fold_copy(fo.at[p, pl.ds(0, 11)], fb.at[:, lon, :], 1, p).start())
        for i in range(11):
            fb[i, pl.ds(lon, 1), :] = fo[lon, pl.ds(i, 1), :]

    @pl.when(has_south)
    def _():
        to_north.wait_recv()
        to_north_too.wait_recv()

    @pl.when(has_north)
    def _():
        to_south.wait_recv()

    to_east.wait_recv()
    to_west.wait_recv()
    later_east.wait_recv()
    later_west.wait_recv()

    for t in range(2):
        for l in range(2):
            at = 2 * t + l
            own, there = row_s[at], from_s[at]
            edge[at] = from_s[8 + l] * (own - there)
            edge[8 + at] = from_s[4 + at] + from_s[12 + l] * own
            own, there = row_n[at], from_n[at]
            edge[4 + at] = row_n[12 + l] * there
            ghost = from_n[4 + at] + row_n[8 + l] * (there - own)
            edge[12 + at] = jnp.where(is_top, 0.0, ghost)

    for r in range(tiles):
        rr = pl.ds(8 * r, 8)
        got = from_w[rr, :]
        own = col_w[rr, :]
        face = moved(got, LANES - both)
        ghost = next_from_w[rr, :] + moved(got, LANES - 2 * both) * own
        next_from_w[rr, :] = ghost
        add_w[rr, :] = face * (own - got)
        got = from_e[rr, :]
        mine = col_e[rr, :]
        ghost = next_from_e[rr, :] + moved(mine, LANES - both) * (got - mine)
        next_from_e[rr, :] = ghost
        add_e[rr, :] = moved(mine, LANES - 2 * both) * got

    def complete(c, carry):
        for j in range(CHUNK):
            k = CHUNK * c + j
            at = pl.ds(k, 1)
            for l in range(2):
                nmb[k, l, pl.ds(first - 1, 1), :] = from_s[8 + l, at, :]
                for t in range(2):
                    i = 2 * t + l
                    low, high = pl.ds(first, 1), pl.ds(last, 1)
                    a1[t, k + 1, l, low, :] = a1[t, k + 1, l, low, :] + edge[i, at, :]
                    a1[t, k + 1, l, high, :] = a1[t, k + 1, l, high, :] + edge[4 + i, at, :]
                    a1[t, k + 1, l, pl.ds(first - 1, 1), :] = edge[8 + i, at, :]
                    a1[t, k + 1, l, pl.ds(last + 1, 1), :] = edge[12 + i, at, :]
            for r in range(tiles):
                rr, here = pl.ds(8 * r, 8), pl.ds(PAD + 8 * r, 8)
                for t in range(2):
                    q = t * levels + k
                    value = moved(add_w[rr, :], lax.rem(LANES - q, LANES))
                    a1[t, k + 1, 0, here, :] = a1[t, k + 1, 0, here, :] + jnp.where(at_first, value, 0.0)
                    value = moved(add_e[rr, :], LANES - 1 - q)
                    a1[t, k + 1, 1, here, :] = a1[t, k + 1, 1, here, :] + jnp.where(at_last, value, 0.0)
        return carry

    lax.fori_loop(0, chunks, complete, 0)

    def second_step(c, carry):
        step_levels(c, a1, True)
        return carry

    lax.fori_loop(0, chunks, second_step, 0)

    relay_east.wait_recv()
    relay_west.wait_recv()

    def upright(ref, row, base):
        spread = jnp.broadcast_to(ref[pl.ds(row, 1), :], (levels, LANES))
        return jnp.sum(jnp.where(row_lane == row_level + base, spread, 0.0), axis=1, keepdims=True)

    sw, nw, se, ne = tiles_w[0], tiles_w[1], tiles_e[0], tiles_e[1]

    def lane_of(tile, at):
        return tile[:, at : at + 1]

    face_w = [upright(from_w, 0, both), upright(from_w, rows - 1, both)]
    beyond_w, beyond_e = upright(from_w, rows + 7, 0), upright(from_e, rows - 1, 2 * both)
    for t in range(2):
        point = t * levels
        there, above = from_s[2 * t], from_n[2 * t]
        corner = lane_of(sw, 8 + t)
        value = from_s[8] * (lane_of(sw, 11) * (there - corner))
        value = value + face_w[0] * (lane_of(sw, 10) * (upright(from_w, 0, point) - corner))
        edge[2 * t] = jnp.where(row_first, -value, 0.0)
        corner = lane_of(se, t)
        value = from_s[9] * (lane_of(tiles_in[0], 12) * corner)
        value = row_s[8] * (lane_of(se, 2) * (upright(from_e, 0, point) - corner)) - value
        edge[2 * t + 1] = jnp.where(row_last, value, 0.0)
        corner = lane_of(nw, 8 + t)
        value = row_n[12] * (lane_of(nw, 11) * (above - corner)) - face_w[1] * (beyond_w * corner)
        edge[4 + 2 * t] = jnp.where(row_first, value, 0.0)
        corner = lane_of(ne, t)
        value = row_n[13] * (lane_of(tiles_in[1], 12) * corner) + row_n[10] * (beyond_e * corner)
        edge[4 + 2 * t + 1] = jnp.where(row_last, value, 0.0)

    def corners(c, carry):
        for j in range(CHUNK):
            k = CHUNK * c + j
            for t in range(2):
                for l in range(2):
                    for i, row in ((2 * t + l, 0), (4 + 2 * t + l, rows - 1)):
                        at = pl.ds(row, 1)
                        out[t, k, at, halves(l)] = out[t, k, at, halves(l)] + edge[i, pl.ds(k, 1), :]
        return carry

    lax.fori_loop(0, chunks, corners, 0)

    @pl.when(is_top)
    def _():
        fold_back.wait_recv()
        for t in range(2):
            value = [fb[2 * t + l] for l in range(2)]
            beyond = fb[8 + 2 * t]
            left = [moved(x, LANES - 1) for x in value]
            right = [moved(x, 1) for x in value]
            to_e = [jnp.where(row_last, left[1], left[0]), jnp.where(row_last, moved(beyond, LANES - 1), left[1])]
            to_w = [jnp.where(row_first, moved(beyond, 1), right[0]), jnp.where(row_first, right[0], right[1])]
            for l in range(2):
                diag, side, down = last_c[l], last_c[4 + l], last_c[6 + l]
                if l == 0:
                    diag = diag + jnp.where(row_first, face_w[1], 0.0)
                    side = side + jnp.where(row_first, face_w[1], 0.0)
                total = diag * value[l] + last_c[2 + l] * to_e[l] - side * to_w[l]
                total = total + down * pltpu.roll(value[l], levels - 1, 0)
                total = total + pltpu.roll(down, 1, 0) * pltpu.roll(value[l], 1, 0)
                edge[8 + 2 * t + l] = total + fb[4 + 2 * t + l]
                edge[12 + 2 * t + l] = last_c[8 + l] * value[l]

        def add(c, carry):
            for j in range(CHUNK):
                k = CHUNK * c + j
                for t in range(2):
                    for l in range(2):
                        for i, row in ((8 + 2 * t + l, rows - 1), (12 + 2 * t + l, rows - 2)):
                            at = pl.ds(row, 1)
                            out[t, k, at, halves(l)] = out[t, k, at, halves(l)] + edge[i, pl.ds(k, 1), :]
            return carry

        lax.fori_loop(0, chunks, add, 0)

    to_east.wait_send()
    to_west.wait_send()
    later_east.wait_send()
    later_west.wait_send()
    relay_east.wait_send()
    relay_west.wait_send()

    @pl.when(has_north)
    def _():
        to_north.wait_send()
        to_north_too.wait_send()
        tile_north.wait_send()
        fold_load.wait()

    @pl.when(has_south)
    def _():
        to_south.wait_send()
        tile_south.wait_send()

    @pl.when(is_top)
    def _():
        fold_out.wait_send()
        fold_back.wait_send()


def per_device(n_lon, n_lat, *args):
    _, levels, rows, cols = args[0].shape
    f32, i32 = jnp.float32, jnp.int32
    field = (levels, rows, cols)
    padded = (2, levels + 2, 2, rows + 2 * PAD, LANES)
    args = [pltpu.with_memory_space_constraint(value, pltpu.HBM) for value in args]
    column = (rows, LANES)
    return pl.pallas_call(
        functools.partial(kernel, n_lon, n_lat),
        out_shape=jax.ShapeDtypeStruct(args[0].shape, f32),
        in_specs=[pl.BlockSpec(memory_space=pltpu.HBM)] * 9,
        out_specs=pl.BlockSpec(memory_space=pltpu.VMEM),
        scratch_shapes=[
            pltpu.VMEM(padded, f32),
            pltpu.VMEM(padded, f32),
            pltpu.VMEM((levels, 2, rows + 2 * PAD, LANES), f32),
            *[pltpu.VMEM(field, f32) for _ in range(4)],
            *[pltpu.VMEM((rows, cols), i32) for _ in range(3)],
            pltpu.SMEM((cols,), i32),
            pltpu.VMEM((4, 2, levels, cols), f32),
            pltpu.VMEM((2, levels, cols), f32),
            pltpu.VMEM((3, levels, cols), f32),
            pltpu.VMEM((3, levels, cols), f32),
            pltpu.VMEM((2, levels, cols), f32),
            *[pltpu.VMEM(field, f32) for _ in range(4)],
            pltpu.VMEM((levels + 1, rows, cols), f32),
            pltpu.VMEM((14, levels, LANES), f32),
            pltpu.VMEM((9, levels, LANES), f32),
            pltpu.VMEM((14, levels, LANES), f32),
            pltpu.VMEM((9, levels, LANES), f32),
            pltpu.VMEM((rows + 8, LANES), f32),
            pltpu.VMEM(column, f32),
            pltpu.VMEM((rows + 8, LANES), f32),
            *[pltpu.VMEM(column, f32) for _ in range(5)],
            *[pltpu.VMEM((2, levels, LANES), f32) for _ in range(4)],
            pltpu.VMEM((16, levels, LANES), f32),
            pltpu.VMEM((10, levels, LANES), f32),
            pltpu.VMEM(column, f32),
            pltpu.VMEM(column, f32),
            pltpu.VMEM((n_lon, 16, LANES), f32),
            pltpu.VMEM((n_lon, 16, LANES), f32),
            *[pltpu.VMEM((n_lon, 8, LANES), f32) for _ in range(6)],
            pltpu.VMEM((n_lon, 16, LANES), f32),
            pltpu.VMEM((11, n_lon, LANES), f32),
            pltpu.SemaphoreType.DMA((18 + 6 * (levels // CHUNK),)),
            pltpu.SemaphoreType.DMA((11,)),
            pltpu.SemaphoreType.DMA((11,)),
            pltpu.SemaphoreType.DMA((2,)),
            pltpu.SemaphoreType.DMA((2,)),
        ],
        compiler_params=pltpu.CompilerParams(
            collective_id=0, has_side_effects=True, vmem_limit_bytes=32 * 1024 * 1024
        ),
    )(*args)


def solution(mesh):
    n_lon, n_lat = mesh.shape["lon"], mesh.shape["lat"]
    placed = (
        P(None, None, "lat", "lon"),
        P(None, "lat", "lon"),
        P(None, "lat", "lon"),
        P(None, "lat", "lon"),
        P(None, "lat", "lon"),
        P("lat", "lon"),
        P("lat", "lon"),
        P("lat", "lon"),
        P("lon"),
    )
    return jax.shard_map(
        functools.partial(per_device, n_lon, n_lat),
        mesh=mesh,
        in_specs=placed,
        out_specs=P(None, None, "lat", "lon"),
        check_vma=False,
    )
```

```python
import functools

import jax
import jax.numpy as jnp
from jax import lax
from jax.experimental import pallas as pl
from jax.experimental.pallas import tpu as pltpu
from jax.sharding import PartitionSpec as P

LANES = 128
PAD = 8
CHUNK = 4
MESH = pl.DeviceIdType.MESH


def kernel(
    n_lon, n_lat,
    ct, u_hbm, v_hbm, d_hbm, w_hbm, cm_hbm, em_hbm, nm_hbm, fp_hbm,
    out,
    a0, a1, nmb, ub, vb, db, wb, cmb, emb, nkb, fps,
    ctr, ur, vr, dr, wr,
    east_c, west_c, north_c, diag_c, down_c,
    row_n, row_s, from_s, from_n,
    col_e, col_w, from_w, from_e, next_e, next_w, next_from_w, next_from_e,
    tiles_out, tiles_in, tiles_w, tiles_e,
    edge, last_c, add_w, add_e,
    fg, fq, fx, fy, gx, gy, f1, f2, fo, fb,
    load_sem, send_sem, recv_sem, fold_send, fold_recv,
):
    _, levels, rows, cols = ct.shape
    lon, lat = lax.axis_index("lon"), lax.axis_index("lat")
    east, west = lax.rem(lon + 1, n_lon), lax.rem(lon + n_lon - 1, n_lon)
    is_top, is_bottom = lat == n_lat - 1, lat == 0
    has_north, has_south = jnp.logical_not(is_top), jnp.logical_not(is_bottom)
    tiles = rows // 8
    first, last = PAD, PAD + rows - 1
    both = 2 * levels
    chunks = levels // CHUNK

    barrier = pltpu.get_barrier_semaphore()

    def greet(at):
        pl.semaphore_signal(barrier, inc=1, device_id=at, device_id_type=MESH)

    def others(body):
        def one(i, carry):
            body(lax.rem(lon + i, n_lon))
            return carry

        lax.fori_loop(1, n_lon, one, 0)

    @pl.when(is_top)
    def _():
        others(lambda p: greet((p, lat)))

    origin = jnp.logical_and(lon == 0, lat == 0)
    east_of = jnp.logical_and(lon == 1, lat == 0)
    west_of = jnp.logical_and(lon == n_lon - 1, lat == 0)

    @pl.when(has_north)
    def _():
        greet((lon, lat + 1))

    @pl.when(jnp.logical_and(has_north, jnp.logical_not(origin)))
    def _():
        greet((east, lat))
        greet((west, lat))

    @pl.when(has_south)
    def _():
        greet((lon, lat - 1))

    def load(src, dst, sem):
        copy = pltpu.make_async_copy(src, dst, load_sem.at[sem])
        copy.start()
        return copy

    tops = (0, 1, rows - 2, rows - 1)
    row_loads = [load(cm_hbm, cmb, 0), load(em_hbm, emb, 1), load(nm_hbm, nkb, 2)]
    for i, row in enumerate(tops):
        row_loads.append(load(ct.at[:, :, row, :], ctr.at[i], 3 + i))
    for i, row in enumerate((0, rows - 1)):
        row_loads.append(load(u_hbm.at[:, row, :], ur.at[i], 7 + i))
        row_loads.append(load(w_hbm.at[:, row, :], wr.at[i], 9 + i))
    for i, row in enumerate((0, rows - 2, rows - 1)):
        row_loads.append(load(v_hbm.at[:, row, :], vr.at[i], 11 + i))
        row_loads.append(load(d_hbm.at[:, row, :], dr.at[i], 14 + i))
    fold_load = load(fp_hbm, fps, 17)

    def chunk_loads(c):
        span = pl.ds(CHUNK * c, CHUNK)
        base = 18 + 6 * c
        pairs = [
            (
                ct.at[:, span, :, pl.ds(LANES * l, LANES)],
                a0.at[:, pl.ds(CHUNK * c + 1, CHUNK), l, pl.ds(PAD, rows), :],
            )
            for l in range(2)
        ]
        pairs += [(src.at[span], dst.at[span]) for src, dst in ((u_hbm, ub), (d_hbm, db), (v_hbm, vb), (w_hbm, wb))]
        return [pltpu.make_async_copy(src, dst, load_sem.at[base + i]) for i, (src, dst) in enumerate(pairs)]

    for c in range(chunks):
        for copy in chunk_loads(c):
            copy.start()

    block = jnp.zeros((rows, LANES), jnp.float32)
    line = jnp.zeros((1, LANES), jnp.float32)
    for buf in (a0, a1):
        for t in range(2):
            for k in (0, levels + 1):
                for l in range(2):
                    buf[t, k, l, pl.ds(PAD, rows), :] = block
    for l in range(2):
        down_c[0, :, LANES * l : LANES * (l + 1)] = block

    def clear(k, carry):
        for l in range(2):
            nmb[k, l, pl.ds(first - 1, 1), :] = line
            for t in range(2):
                a0[t, k + 1, l, pl.ds(first - 1, 1), :] = line
                a0[t, k + 1, l, pl.ds(last + 1, 1), :] = line
        return carry

    lax.fori_loop(0, levels, clear, 0)

    @pl.when(is_bottom)
    def _():
        from_s[...] = jnp.zeros_like(from_s)
        tiles_in[0] = jnp.zeros((levels, LANES), jnp.float32)

    @pl.when(is_top)
    def _():
        from_n[...] = jnp.zeros_like(from_n)
        tiles_in[1] = jnp.zeros((levels, LANES), jnp.float32)

    lane = lax.broadcasted_iota(jnp.int32, (8, LANES), 1)
    sub = lax.broadcasted_iota(jnp.int32, (8, LANES), 0)
    at_first, at_last = lane == 0, lane == LANES - 1
    row_lane = lax.broadcasted_iota(jnp.int32, (levels, LANES), 1)
    row_level = lax.broadcasted_iota(jnp.int32, (levels, LANES), 0)
    row_first, row_last = row_lane == 0, row_lane == LANES - 1

    def moved(value, by):
        return pltpu.roll(value, by, 1)

    def halves(l):
        return slice(LANES * l, LANES * (l + 1))

    for copy in row_loads:
        copy.wait()

    def bits(buf, row, count=1):
        mask = jnp.left_shift(jnp.full((levels, LANES), 2**count - 1, jnp.int32), row_level)
        return [jnp.bitwise_and(jnp.broadcast_to(buf[pl.ds(row, 1), halves(l)], mask.shape), mask) == mask for l in range(2)]

    def edge_row(i, row):
        at = 3 * i
        cell = [ctr[at, t] for t in range(2)]
        inner = [ctr[1 + i, t] for t in range(2)]
        open_e, open_n, open_c, open_d = bits(emb, row), bits(nkb, row), bits(cmb, row), bits(cmb, row, 2)
        plus, minus, north, south, diag, down = [], [], [], [], [], []
        for l in range(2):
            half, diff = 0.5 * ur[i, :, halves(l)], dr[2 * i, :, halves(l)]
            plus.append(jnp.where(open_e[l], half + diff, 0.0))
            minus.append(jnp.where(open_e[l], half - diff, 0.0))
            half = 0.5 * vr[2 * i, :, halves(l)]
            north.append(jnp.where(open_n[l], half + diff, 0.0))
            south.append(jnp.where(open_n[l], half - diff, 0.0))
            down.append(jnp.where(open_d[l], wr[i, :, halves(l)], 0.0))
        turned = [moved(x, 1) for x in minus]
        side = [jnp.where(row_first, 0.0, turned[0]), jnp.where(row_first, turned[0], turned[1])]
        if i == 1:
            open_b = bits(nkb, row - 1)
            beyond = [jnp.where(open_b[l], 0.5 * vr[1, :, halves(l)] - dr[1, :, halves(l)], 0.0) for l in range(2)]
        result = [[None, None], [None, None]]
        for l in range(2):
            up = pltpu.roll(down[l], 1, 0)
            diag = jnp.where(open_c[l], 1.0, 0.0) - plus[l] - north[l] - down[l] - up + side[l]
            if i == 1:
                diag = diag + beyond[l]
                last_c[l], last_c[2 + l], last_c[4 + l], last_c[6 + l] = diag, plus[l], side[l], down[l]
                last_c[8 + l] = jnp.where(open_b[l], 0.5 * vr[1, :, halves(l)] + dr[1, :, halves(l)], 0.0)
            for t in range(2):
                here = cell[t][:, halves(l)]
                left = [moved(cell[t][:, halves(m)], LANES - 1) for m in range(2)]
                right = [moved(cell[t][:, halves(m)], 1) for m in range(2)]
                to_e = jnp.where(row_last, left[1], left[0]) if l == 0 else jnp.where(row_last, 0.0, left[1])
                to_w = right[0] if l == 0 else jnp.where(row_first, right[0], right[1])
                total = diag * here + plus[l] * to_e - side[l] * to_w
                total = total + down[l] * pltpu.roll(here, levels - 1, 0) + up * pltpu.roll(here, 1, 0)
                if i == 0:
                    total = total + north[l] * inner[t][:, halves(l)]
                else:
                    total = total - beyond[l] * inner[t][:, halves(l)]
                result[t][l] = total
        return cell, result, plus, minus, north, south

    cell, result, plus, minus, north, south = edge_row(1, rows - 1)
    for l in range(2):
        for t in range(2):
            row_n[2 * t + l] = cell[t][:, halves(l)]
            row_n[4 + 2 * t + l] = result[t][l]
        row_n[8 + l] = south[l]
        row_n[12 + l] = north[l]
    row_n[10] = plus[1]
    row_n[11] = minus[1]

    def corner_tile(cell, minus, plus, south):
        tile = jnp.zeros((levels, LANES), jnp.float32)
        for to, value, at in (
            (0, cell[0][:, halves(0)], 0), (1, cell[1][:, halves(0)], 0), (2, south[0], 0),
            (8, cell[0][:, halves(1)], LANES - 1), (9, cell[1][:, halves(1)], LANES - 1), (10, south[1], LANES - 1),
            (11, minus[1], LANES - 1), (12, plus[1], LANES - 1),
        ):
            tile = jnp.where(row_lane == to, moved(value, (to - at) % LANES), tile)
        return tile

    tiles_out[0] = corner_tile(cell, minus, plus, south)
    cell, result, plus, minus, north, south = edge_row(0, 0)
    for l in range(2):
        for t in range(2):
            row_s[2 * t + l] = cell[t][:, halves(l)]
            row_s[4 + 2 * t + l] = result[t][l]
    row_s[8] = plus[1]
    tiles_out[1] = corner_tile(cell, minus, plus, south)

    def remote(src, dst, sem, at):
        return pltpu.make_async_remote_copy(
            src_ref=src, dst_ref=dst, send_sem=send_sem.at[sem], recv_sem=recv_sem.at[sem],
            device_id=at, device_id_type=MESH,
        )

    to_north = remote(row_n.at[pl.ds(0, 10)], from_s.at[pl.ds(0, 10)], 0, (lon, lat + 1))
    to_north_too = remote(row_n.at[pl.ds(12, 2)], from_s.at[pl.ds(12, 2)], 10, (lon, lat + 1))
    to_south = remote(row_s.at[pl.ds(0, 8)], from_n.at[pl.ds(0, 8)], 1, (lon, lat - 1))
    to_east = remote(col_e, from_w, 2, (east, lat))
    to_west = remote(col_w, from_e, 3, (west, lat))
    later_east = remote(next_e, next_from_w, 4, (east, lat))
    later_west = remote(next_w, next_from_e, 5, (west, lat))
    tail = pl.ds(rows - 8, 8)
    tile_north = remote(tiles_out.at[0], tiles_in.at[0], 6, (lon, lat + 1))
    tile_south = remote(tiles_out.at[1], tiles_in.at[1], 7, (lon, lat - 1))
    relay_east = remote(tiles_in, tiles_w, 8, (east, lat))
    relay_west = remote(tiles_in, tiles_e, 9, (west, lat))

    def fold_copy(src, dst, sem, at):
        return pltpu.make_async_remote_copy(
            src_ref=src, dst_ref=dst, send_sem=fold_send.at[sem], recv_sem=fold_recv.at[sem],
            device_id=(at, lat), device_id_type=MESH,
        )

    some = pl.ds(0, n_lon - 1)
    fold_out = fold_copy(fq.at[some, pl.ds(0, 12)], fg.at[some, pl.ds(0, 12)], 0, east)
    fold_back = fold_copy(fo.at[some, pl.ds(0, 11)], fb.at[:, some, :], 1, east)

    def first_sends():
        count = 2 + jnp.where(is_top, n_lon - 3, 1) + jnp.where(is_bottom, 0, 1)
        count = count - jnp.where(jnp.logical_or(east_of, west_of), 1, 0)
        pl.semaphore_wait(barrier, count)

        @pl.when(is_top)
        def _():
            others(lambda p: fold_copy(fq.at[p, pl.ds(0, 12)], fg.at[lon, pl.ds(0, 12)], 0, p).start())
            fg[lon] = fq[lon]

        @pl.when(has_north)
        def _():
            tile_north.start()
            to_north.start()
            to_north_too.start()

        @pl.when(has_south)
        def _():
            tile_south.start()
            to_south.start()

    @pl.when(is_top)
    def _():
        def collect(k, carry):
            for i in range(12):
                fq[k, pl.ds(i, 1), :] = row_n[i, pl.ds(k, 1), :]
            return carry

        lax.fori_loop(0, levels, collect, 0)

    ahead = jnp.logical_and(lat <= 1, jnp.logical_or(lon <= 1, lon == n_lon - 1))
    ahead = jnp.logical_and(ahead, jnp.logical_or(lon > 0, lat > 0))

    @pl.when(jnp.logical_not(ahead))
    def _():
        first_sends()

    col_e[...] = jnp.zeros_like(col_e)
    col_w[...] = jnp.zeros_like(col_w)

    def coefficients(c, carry):
        for copy in chunk_loads(c):
            copy.wait()
        for r in range(tiles):
            rr, pr = pl.ds(8 * r, 8), pl.ds(PAD + 8 * r, 8)
            pack_e, pack_w = col_e[rr, :], col_w[rr, :]
            for j in range(CHUNK):
                k = CHUNK * c + j
                bit = jnp.left_shift(jnp.int32(1), k)
                pair = jnp.left_shift(jnp.int32(3), k)
                minus, plus, norths, souths = [], [], [], []
                for l in range(2):
                    cc = halves(l)
                    half, diff = 0.5 * ub[k, rr, cc], db[k, rr, cc]
                    open_e = jnp.bitwise_and(emb[rr, cc], bit) != 0
                    plus.append(jnp.where(open_e, half + diff, 0.0))
                    minus.append(jnp.where(open_e, half - diff, 0.0))
                    half = 0.5 * vb[k, rr, cc]
                    open_n = jnp.bitwise_and(nkb[rr, cc], bit) != 0
                    norths.append(jnp.where(open_n, half + diff, 0.0))
                    souths.append(jnp.where(open_n, half - diff, 0.0))
                turned = [moved(x, 1) for x in minus]
                side = [jnp.where(at_first, 0.0, turned[0]), jnp.where(at_first, turned[0], turned[1])]
                for l in range(2):
                    cc = halves(l)
                    cells = cmb[rr, cc]
                    down = jnp.where(jnp.bitwise_and(cells, pair) == pair, wb[k, rr, cc], 0.0)
                    east_c[k, rr, cc] = plus[l]
                    west_c[k, rr, cc] = side[l]
                    north_c[k, rr, cc] = norths[l]
                    nmb[k, l, pr, :] = souths[l]
                    down_c[k + 1, rr, cc] = down
                    here = jnp.where(jnp.bitwise_and(cells, bit) != 0, 1.0, 0.0)
                    below = nmb[k, l, pl.ds(PAD + 8 * r - 1, 8), :]
                    diag_c[k, rr, cc] = here - plus[l] - norths[l] - down - down_c[k, rr, cc] + side[l] + below

                def put(pack, value, lane_to, lane_from):
                    return jnp.where(lane == lane_to, moved(value, lax.rem(lane_to + LANES - lane_from, LANES)), pack)

                for t in range(2):
                    pack_e = put(pack_e, a0[t, k + 1, 1, pr, :], t * levels + k, LANES - 1)
                    pack_w = put(pack_w, a0[t, k + 1, 0, pr, :], t * levels + k, 0)
                pack_e = put(pack_e, minus[1], both + k, LANES - 1)
                pack_e = put(pack_e, plus[1], 2 * both + k, LANES - 1)
                if r == tiles - 1:
                    pack_e = put(pack_e, souths[1], 3 * both + k, LANES - 1)
                    pack_w = put(pack_w, souths[0], both + k, 0)
                    pack_w = put(pack_w, norths[0], 2 * both + k, 0)
                    extra = pl.ds(rows, 8)
                    col_e[extra, :] = put(col_e[extra, :], norths[1], k, LANES - 1)
            col_e[rr, :] = pack_e
            col_w[rr, :] = pack_w
        return carry

    lax.fori_loop(0, chunks, coefficients, 0)

    def doubled(pack, starts):
        again = moved(pack, levels)
        for start in starts:
            pack = jnp.where(jnp.logical_and(lane >= start + levels, lane < start + both), again, pack)
        return pack

    for r in range(tiles):
        rr = pl.ds(8 * r, 8)
        col_e[rr, :] = doubled(col_e[rr, :], (both, 2 * both, 3 * both))
    extra = pl.ds(rows, 8)
    col_e[extra, :] = doubled(col_e[extra, :], (0,))
    col_w[tail, :] = doubled(col_w[tail, :], (both, 2 * both))

    def column_sends():
        @pl.when(jnp.logical_not(west_of))
        def _():
            to_east.start()

        @pl.when(jnp.logical_not(east_of))
        def _():
            to_west.start()

    @pl.when(jnp.logical_not(ahead))
    def _():
        column_sends()

    def step_levels(c, buf, second):
        for r in range(tiles):
            rr, here = pl.ds(8 * r, 8), pl.ds(PAD + 8 * r, 8)
            above, below = pl.ds(PAD + 8 * r + 1, 8), pl.ds(PAD + 8 * r - 1, 8)
            column = [
                [[buf[t, CHUNK * c + j, l, here, :] for j in range(CHUNK + 2)] for l in range(2)] for t in range(2)
            ]
            downs = [[down_c[CHUNK * c + j, rr, halves(l)] for j in range(CHUNK + 1)] for l in range(2)]
            if second:
                ghost_w, ghost_e, face_w = next_from_w[rr, :], next_from_e[rr, :], from_w[rr, :]
            for j in range(CHUNK):
                k = CHUNK * c + j
                to_e, to_w = [], []
                for t in range(2):
                    q = t * levels + k
                    value = [column[t][l][j + 1] for l in range(2)]
                    left = [moved(x, LANES - 1) for x in value]
                    right = [moved(x, 1) for x in value]
                    edge_e = moved(ghost_e, LANES - 1 - q) if second else 0.0
                    to_e.append([jnp.where(at_last, left[1], left[0]), jnp.where(at_last, edge_e, left[1])])
                    edge_w = jnp.where(at_first, moved(ghost_w, lax.rem(LANES - q, LANES)), right[0]) if second else right[0]
                    to_w.append([edge_w, jnp.where(at_first, right[0], right[1])])
                for l in range(2):
                    cc = halves(l)
                    ce, cw, cn, cs = east_c[k, rr, cc], west_c[k, rr, cc], north_c[k, rr, cc], nmb[k, l, below, :]
                    cx = diag_c[k, rr, cc]
                    if second and l == 0:
                        face = jnp.where(at_first, moved(face_w, LANES - both - k), 0.0)
                        cw, cx = cw + face, cx + face
                    if second and r == 0:
                        cx = cx + jnp.where(sub == 0, cs, 0.0)
                    for t in range(2):
                        total = cx * column[t][l][j + 1] + ce * to_e[t][l] - cw * to_w[t][l]
                        total = total + (cn * buf[t, k + 1, l, above, :] - cs * buf[t, k + 1, l, below, :])
                        total = total + (downs[l][j + 1] * column[t][l][j + 2] + downs[l][j] * column[t][l][j])
                        if second:
                            out[t, k, rr, cc] = total
                        else:
                            a1[t, k + 1, l, here, :] = total

    def first_step(c, carry):
        step_levels(c, a0, False)
        return carry

    lax.fori_loop(0, chunks, first_step, 0)

    def pack_result(c, packs):
        packs = list(packs)
        for j in range(CHUNK):
            k = CHUNK * c + j
            for t in range(2):
                q = t * levels + k
                for r in range(tiles):
                    here = pl.ds(PAD + 8 * r, 8)
                    packs[r] = jnp.where(lane == q, moved(a1[t, k + 1, 1, here, :], q + 1), packs[r])
                    packs[tiles + r] = jnp.where(lane == q, moved(a1[t, k + 1, 0, here, :], q), packs[tiles + r])
        return tuple(packs)

    packs = lax.fori_loop(0, chunks, pack_result, tuple(jnp.zeros((8, LANES), jnp.float32) for _ in range(2 * tiles)))
    for r in range(tiles):
        next_e[pl.ds(8 * r, 8), :] = packs[r]
        next_w[pl.ds(8 * r, 8), :] = packs[tiles + r]
    @pl.when(ahead)
    def _():
        first_sends()
        column_sends()

    @pl.when(jnp.logical_not(west_of))
    def _():
        later_east.start()

    @pl.when(jnp.logical_not(east_of))
    def _():
        later_west.start()

    @pl.when(has_south)
    def _():
        tile_north.wait_recv()

    @pl.when(has_north)
    def _():
        tile_south.wait_recv()

    @pl.when(jnp.logical_not(west_of))
    def _():
        relay_east.start()

    @pl.when(jnp.logical_not(east_of))
    def _():
        relay_west.start()

    even = jnp.bitwise_and(sub, 1) == 0

    @pl.when(is_top)
    def _():
        fold_load.wait()
        fold_out.wait_recv()
        fixed = lax.rem(fps[0] + lon * cols, n_lon * cols)
        tile = fixed // LANES
        home, odd = tile // 2, lax.rem(tile, 2)
        within = lax.rem(fixed, LANES)
        source = jnp.bitwise_and(within - lane, LANES - 1)
        keep = jnp.logical_xor(lane <= within, jnp.broadcast_to(odd, lane.shape) == 1)

        def faces(j, at):
            shape = (8, LANES)
            return jnp.where(
                even,
                jnp.broadcast_to(fg[j, pl.ds(at, 1), :], shape),
                jnp.broadcast_to(fg[j, pl.ds(at + 1, 1), :], shape),
            )

        def turn(j, value, straight, swapped):
            turned = jnp.take_along_axis(value, source, axis=1, mode="promise_in_bounds")
            straight[j] = turned
            swapped[j] = jnp.where(even, pltpu.roll(turned, 7, 0), pltpu.roll(turned, 1, 0))

        def turned(i, straight, swapped):
            here = lax.rem(home + n_lon - i, n_lon)
            before = lax.rem(home + 2 * n_lon - i - 1, n_lon)
            third = lax.rem(home + 2 * n_lon - i - 1 + odd, n_lon)
            return jnp.where(keep, jnp.where(even, straight[here], straight[before]), swapped[third])

        low = sub < 4
        for j in range(n_lon):
            e, w = (j + 1) % n_lon, (j - 1) % n_lon
            own = fg[j, pl.ds(0, 8), :]
            face = faces(j, 8)
            to_w = pltpu.roll(moved(fg[w, pl.ds(0, 8), :], 1), 7, 0)
            to_e = pltpu.roll(moved(fg[e, pl.ds(0, 8), :], LANES - 1), 1, 0)
            face_w = moved(jnp.broadcast_to(fg[w, pl.ds(11, 1), :], (8, LANES)), 1)
            face_e = jnp.broadcast_to(fg[j, pl.ds(10, 1), :], (8, LANES))
            inner = jnp.where(jnp.logical_and(even, at_first), face_w * (own - to_w), 0.0)
            inner = inner + jnp.where(jnp.logical_and(jnp.logical_not(even), at_last), face_e * to_e, 0.0)
            value = -(face * jnp.where(low, own, own + pltpu.roll(inner, 4, 0)))
            f2[j] = value
            turn(j, value, fx, fy)
            turn(j, face, gx, gy)
        for i in range(n_lon):
            value = turned(i, fx, fy)
            f1[i] = value
            later = value - turned(i, gx, gy) * pltpu.roll(f2[i], 4, 0)
            fo[i, pl.ds(0, 8), :] = jnp.where(low, value, later)
        for i in range(n_lon):
            e, w = (i + 1) % n_lon, (i - 1) % n_lon
            fo[i, pl.ds(8, 8), :] = jnp.where(at_last, pltpu.roll(f1[w], 7, 0), f1[e])
        others(lambda p: fold_copy(fo.at[p, pl.ds(0, 11)], fb.at[:, lon, :], 1, p).start())
        for i in range(11):
            fb[i, pl.ds(lon, 1), :] = fo[lon, pl.ds(i, 1), :]

    to_east.wait_recv()

    @pl.when(east_of)
    def _():
        to_west.start()
        later_west.start()
        relay_west.start()

    to_west.wait_recv()

    @pl.when(west_of)
    def _():
        to_east.start()
        later_east.start()
        relay_east.start()

    @pl.when(has_south)
    def _():
        to_north.wait_recv()
        to_north_too.wait_recv()

    @pl.when(has_north)
    def _():
        to_south.wait_recv()

    later_east.wait_recv()
    later_west.wait_recv()

    for t in range(2):
        for l in range(2):
            at = 2 * t + l
            own, there = row_s[at], from_s[at]
            edge[at] = from_s[8 + l] * (own - there)
            edge[8 + at] = from_s[4 + at] + from_s[12 + l] * own
            own, there = row_n[at], from_n[at]
            edge[4 + at] = row_n[12 + l] * there
            ghost = from_n[4 + at] + row_n[8 + l] * (there - own)
            edge[12 + at] = jnp.where(is_top, 0.0, ghost)

    for r in range(tiles):
        rr = pl.ds(8 * r, 8)
        got = from_w[rr, :]
        own = col_w[rr, :]
        face = moved(got, LANES - both)
        ghost = next_from_w[rr, :] + moved(got, LANES - 2 * both) * own
        next_from_w[rr, :] = ghost
        add_w[rr, :] = face * (own - got)
        got = from_e[rr, :]
        mine = col_e[rr, :]
        ghost = next_from_e[rr, :] + moved(mine, LANES - both) * (got - mine)
        next_from_e[rr, :] = ghost
        add_e[rr, :] = moved(mine, LANES - 2 * both) * got

    def complete(c, carry):
        for j in range(CHUNK):
            k = CHUNK * c + j
            at = pl.ds(k, 1)
            for l in range(2):
                nmb[k, l, pl.ds(first - 1, 1), :] = from_s[8 + l, at, :]
                for t in range(2):
                    i = 2 * t + l
                    low, high = pl.ds(first, 1), pl.ds(last, 1)
                    a1[t, k + 1, l, low, :] = a1[t, k + 1, l, low, :] + edge[i, at, :]
                    a1[t, k + 1, l, high, :] = a1[t, k + 1, l, high, :] + edge[4 + i, at, :]
                    a1[t, k + 1, l, pl.ds(first - 1, 1), :] = edge[8 + i, at, :]
                    a1[t, k + 1, l, pl.ds(last + 1, 1), :] = edge[12 + i, at, :]
            for r in range(tiles):
                rr, here = pl.ds(8 * r, 8), pl.ds(PAD + 8 * r, 8)
                for t in range(2):
                    q = t * levels + k
                    value = moved(add_w[rr, :], lax.rem(LANES - q, LANES))
                    a1[t, k + 1, 0, here, :] = a1[t, k + 1, 0, here, :] + jnp.where(at_first, value, 0.0)
                    value = moved(add_e[rr, :], LANES - 1 - q)
                    a1[t, k + 1, 1, here, :] = a1[t, k + 1, 1, here, :] + jnp.where(at_last, value, 0.0)
        return carry

    lax.fori_loop(0, chunks, complete, 0)

    def second_step(c, carry):
        step_levels(c, a1, True)
        return carry

    lax.fori_loop(0, chunks, second_step, 0)

    relay_east.wait_recv()
    relay_west.wait_recv()

    def upright(ref, row, base):
        spread = jnp.broadcast_to(ref[pl.ds(row, 1), :], (levels, LANES))
        return jnp.sum(jnp.where(row_lane == row_level + base, spread, 0.0), axis=1, keepdims=True)

    sw, nw, se, ne = tiles_w[0], tiles_w[1], tiles_e[0], tiles_e[1]

    def lane_of(tile, at):
        return tile[:, at : at + 1]

    face_w = [upright(from_w, 0, both), upright(from_w, rows - 1, both)]
    beyond_w, beyond_e = upright(from_w, rows + 7, 0), upright(from_e, rows - 1, 2 * both)
    for t in range(2):
        point = t * levels
        there, above = from_s[2 * t], from_n[2 * t]
        corner = lane_of(sw, 8 + t)
        value = from_s[8] * (lane_of(sw, 11) * (there - corner))
        value = value + face_w[0] * (lane_of(sw, 10) * (upright(from_w, 0, point) - corner))
        edge[2 * t] = jnp.where(row_first, -value, 0.0)
        corner = lane_of(se, t)
        value = from_s[9] * (lane_of(tiles_in[0], 12) * corner)
        value = row_s[8] * (lane_of(se, 2) * (upright(from_e, 0, point) - corner)) - value
        edge[2 * t + 1] = jnp.where(row_last, value, 0.0)
        corner = lane_of(nw, 8 + t)
        value = row_n[12] * (lane_of(nw, 11) * (above - corner)) - face_w[1] * (beyond_w * corner)
        edge[4 + 2 * t] = jnp.where(row_first, value, 0.0)
        corner = lane_of(ne, t)
        value = row_n[13] * (lane_of(tiles_in[1], 12) * corner) + row_n[10] * (beyond_e * corner)
        edge[4 + 2 * t + 1] = jnp.where(row_last, value, 0.0)

    def corners(c, carry):
        for j in range(CHUNK):
            k = CHUNK * c + j
            for t in range(2):
                for l in range(2):
                    for i, row in ((2 * t + l, 0), (4 + 2 * t + l, rows - 1)):
                        at = pl.ds(row, 1)
                        out[t, k, at, halves(l)] = out[t, k, at, halves(l)] + edge[i, pl.ds(k, 1), :]
        return carry

    lax.fori_loop(0, chunks, corners, 0)

    @pl.when(is_top)
    def _():
        fold_back.wait_recv()
        for t in range(2):
            value = [fb[2 * t + l] for l in range(2)]
            beyond = fb[8 + 2 * t]
            left = [moved(x, LANES - 1) for x in value]
            right = [moved(x, 1) for x in value]
            to_e = [jnp.where(row_last, left[1], left[0]), jnp.where(row_last, moved(beyond, LANES - 1), left[1])]
            to_w = [jnp.where(row_first, moved(beyond, 1), right[0]), jnp.where(row_first, right[0], right[1])]
            for l in range(2):
                diag, side, down = last_c[l], last_c[4 + l], last_c[6 + l]
                if l == 0:
                    diag = diag + jnp.where(row_first, face_w[1], 0.0)
                    side = side + jnp.where(row_first, face_w[1], 0.0)
                total = diag * value[l] + last_c[2 + l] * to_e[l] - side * to_w[l]
                total = total + down * pltpu.roll(value[l], levels - 1, 0)
                total = total + pltpu.roll(down, 1, 0) * pltpu.roll(value[l], 1, 0)
                edge[8 + 2 * t + l] = total + fb[4 + 2 * t + l]
                edge[12 + 2 * t + l] = last_c[8 + l] * value[l]

        def add(c, carry):
            for j in range(CHUNK):
                k = CHUNK * c + j
                for t in range(2):
                    for l in range(2):
                        for i, row in ((8 + 2 * t + l, rows - 1), (12 + 2 * t + l, rows - 2)):
                            at = pl.ds(row, 1)
                            out[t, k, at, halves(l)] = out[t, k, at, halves(l)] + edge[i, pl.ds(k, 1), :]
            return carry

        lax.fori_loop(0, chunks, add, 0)

    to_east.wait_send()
    to_west.wait_send()
    later_east.wait_send()
    later_west.wait_send()
    relay_east.wait_send()
    relay_west.wait_send()

    @pl.when(has_north)
    def _():
        to_north.wait_send()
        to_north_too.wait_send()
        tile_north.wait_send()
        fold_load.wait()

    @pl.when(has_south)
    def _():
        to_south.wait_send()
        tile_south.wait_send()

    @pl.when(is_top)
    def _():
        fold_out.wait_send()
        fold_back.wait_send()


def per_device(n_lon, n_lat, *args):
    _, levels, rows, cols = args[0].shape
    f32, i32 = jnp.float32, jnp.int32
    field = (levels, rows, cols)
    padded = (2, levels + 2, 2, rows + 2 * PAD, LANES)
    args = [pltpu.with_memory_space_constraint(value, pltpu.HBM) for value in args]
    column = (rows, LANES)
    return pl.pallas_call(
        functools.partial(kernel, n_lon, n_lat),
        out_shape=jax.ShapeDtypeStruct(args[0].shape, f32),
        in_specs=[pl.BlockSpec(memory_space=pltpu.HBM)] * 9,
        out_specs=pl.BlockSpec(memory_space=pltpu.VMEM),
        scratch_shapes=[
            pltpu.VMEM(padded, f32),
            pltpu.VMEM(padded, f32),
            pltpu.VMEM((levels, 2, rows + 2 * PAD, LANES), f32),
            *[pltpu.VMEM(field, f32) for _ in range(4)],
            *[pltpu.VMEM((rows, cols), i32) for _ in range(3)],
            pltpu.SMEM((cols,), i32),
            pltpu.VMEM((4, 2, levels, cols), f32),
            pltpu.VMEM((2, levels, cols), f32),
            pltpu.VMEM((3, levels, cols), f32),
            pltpu.VMEM((3, levels, cols), f32),
            pltpu.VMEM((2, levels, cols), f32),
            *[pltpu.VMEM(field, f32) for _ in range(4)],
            pltpu.VMEM((levels + 1, rows, cols), f32),
            pltpu.VMEM((14, levels, LANES), f32),
            pltpu.VMEM((9, levels, LANES), f32),
            pltpu.VMEM((14, levels, LANES), f32),
            pltpu.VMEM((9, levels, LANES), f32),
            pltpu.VMEM((rows + 8, LANES), f32),
            pltpu.VMEM(column, f32),
            pltpu.VMEM((rows + 8, LANES), f32),
            *[pltpu.VMEM(column, f32) for _ in range(5)],
            *[pltpu.VMEM((2, levels, LANES), f32) for _ in range(4)],
            pltpu.VMEM((16, levels, LANES), f32),
            pltpu.VMEM((10, levels, LANES), f32),
            pltpu.VMEM(column, f32),
            pltpu.VMEM(column, f32),
            pltpu.VMEM((n_lon, 16, LANES), f32),
            pltpu.VMEM((n_lon, 16, LANES), f32),
            *[pltpu.VMEM((n_lon, 8, LANES), f32) for _ in range(6)],
            pltpu.VMEM((n_lon, 16, LANES), f32),
            pltpu.VMEM((11, n_lon, LANES), f32),
            pltpu.SemaphoreType.DMA((18 + 6 * (levels // CHUNK),)),
            pltpu.SemaphoreType.DMA((11,)),
            pltpu.SemaphoreType.DMA((11,)),
            pltpu.SemaphoreType.DMA((2,)),
            pltpu.SemaphoreType.DMA((2,)),
        ],
        compiler_params=pltpu.CompilerParams(
            collective_id=0, has_side_effects=True, vmem_limit_bytes=32 * 1024 * 1024
        ),
    )(*args)


def solution(mesh):
    n_lon, n_lat = mesh.shape["lon"], mesh.shape["lat"]
    placed = (
        P(None, None, "lat", "lon"),
        P(None, "lat", "lon"),
        P(None, "lat", "lon"),
        P(None, "lat", "lon"),
        P(None, "lat", "lon"),
        P("lat", "lon"),
        P("lat", "lon"),
        P("lat", "lon"),
        P("lon"),
    )
    return jax.shard_map(
        functools.partial(per_device, n_lon, n_lat),
        mesh=mesh,
        in_specs=placed,
        out_specs=P(None, None, "lat", "lon"),
        check_vma=False,
    )
```
